128 devices in a mesh: clus: 8 (over y, core), pen: 16 (over x, z).
Axes of the slice: x: 4, y: 4, z: 4, core: 2. Of those that a mesh axis runs over, the one named last changes fastest.
Arguments:
- charges: bfloat16 [262144], P(('clus', 'pen')), may hold values from -6 to 6
- stencil: float32 [27, 262144], P(None, ('clus', 'pen')), may hold values from -3 to 3
- corner_cells: int32 [3, 262144], P(None, ('clus', 'pen')), may hold values from 0 to 253, as said below
- cluster_sizes: int32 [1024], P(('clus', 'pen')), may hold values from 1 to 256, as said below
- near_source: int32 [4096], P(('clus', 'pen')), may hold values from 0 to 1023, as said below
- near_blocks: bfloat16 [4096, 256, 256], P(('clus', 'pen')), may hold values from -0.1875 to 0.1875
- green_spectrum: float32 [512, 512, 512], P(None, 'clus', 'pen'), may hold values from 0.05 to 1
Outputs:
- potential: float32 [262144], P(('clus', 'pen'))
The draws below stay inside these ranges and needn't reach their ends.
Inputs may be any that keep to these rules, and one draw needn't show every extreme that they name: `corner_cells`: each stencil box lies in the grid; along the first dimension it lies within the 256 / 8 planes of the clus index that holds the panel. `cluster_sizes`: every device holds a cluster of exactly 256 live panels. `near_source`: the first block of each cluster has the cluster itself as source; the other sources lie on the same or an adjacent clus index.
All inputs are finite; a program needn't handle non-finite values.
Results may differ from the reference program's by a relative error of at most 0.0006.
Values may be sent and summed in bfloat16 or wider, within the bound.
No kernel may reach another device: no remote copies, remote signals or barrier semaphores. Data moves between devices by JAX's collectives and lax.ppermute only.
A program may use at most 128 MiB of HBM per device.

```python
import math
import jax
import jax.numpy as jnp
from jax import lax

M = 256
L = 512
S = 27
CAP = 256
NB = 4
CLU_DEV = 8
CLUSTERS = 1024
PANELS = 262144
PAIRS = 4096
N_CLUS = 8
N_PEN = 16


def draw_corner_cells(key, part):
    key = jax.random.fold_in(key, 11)
    key_first, key_second, key_third = jax.random.split(key, 3)
    total = CLU_DEV * CAP * N_CLUS * N_PEN
    planes = M // N_CLUS
    slab_index = jnp.arange(total, dtype=jnp.int32) // (N_PEN * CLU_DEV * CAP)
    coord_first = slab_index * planes + jax.random.randint(key_first, (total,), 0, planes - 2)
    coord_second = jax.random.randint(key_second, (total,), 0, M - 2)
    coord_third = jax.random.randint(key_third, (total,), 0, M - 2)
    return jnp.stack([coord_first, coord_second, coord_third]).astype(jnp.int32)


def draw_cluster_sizes(key, part):
    key = jax.random.fold_in(key, 12)
    key_level, key_size, key_full = jax.random.split(key, 3)
    devices = N_CLUS * N_PEN
    level = jax.random.randint(key_level, (devices, 1), 1, 5)
    raw_size = jax.random.randint(key_size, (devices, CLU_DEV), 0, CAP)
    sizes = 1 + raw_size * level // 4
    full_slot = jax.random.randint(key_full, (devices, 1), 0, CLU_DEV)
    column = jnp.arange(CLU_DEV, dtype=jnp.int32)[None, :]
    sizes = jnp.where(column == full_slot, CAP, sizes)
    return sizes.reshape(-1).astype(jnp.int32)


def draw_near_source(key, part):
    key = jax.random.fold_in(key, 13)
    key_shift, key_row, key_slot = jax.random.split(key, 3)
    total = CLU_DEV * N_CLUS * N_PEN * NB
    pair_index = jnp.arange(total, dtype=jnp.int32)
    target = pair_index // NB
    slab_index = target // (CLU_DEV * N_PEN)
    shifted = jnp.clip(slab_index + jax.random.randint(key_shift, (total,), -1, 2), 0, N_CLUS - 1)
    row_pick = jax.random.randint(key_row, (total,), 0, N_PEN)
    slot_pick = jax.random.randint(key_slot, (total,), 0, CLU_DEV)
    source = (shifted * N_PEN + row_pick) * CLU_DEV + slot_pick
    return jnp.where(pair_index % NB == 0, target, source).astype(jnp.int32)


def shard_levels(own_key, extent, cuts, smallest, largest):
    def one(axis_at, parts):
        heights = jax.random.uniform(jax.random.fold_in(jax.random.fold_in(own_key, 6), axis_at), (parts,), jnp.float32, smallest / len(cuts), largest / len(cuts))
        return jnp.repeat(jnp.exp(heights), extent[axis_at] // parts).reshape((-1,) + (1,) * (len(extent) - axis_at - 1))

    factor_of = one(*cuts[0])
    for cut in cuts[1:]:
        factor_of = factor_of * one(*cut)
    return factor_of


def bell_draw(own_key, dims, width, limit, cuts=(), held_as=jnp.bfloat16):
    array = jax.random.normal(own_key, dims, jnp.float32) * width
    if len(cuts) > 0:
        array = shard_levels(own_key, dims, cuts, -0.22, 0.18) * array
    return jnp.clip(array, min=-limit, max=limit).astype(held_as)


def setup_inputs(seed: int = 0) -> dict:
    seeds = jax.random.split(jax.random.key(seed), 8)
    charges = bell_draw(seeds[0], (PANELS,), 1.0, 6.0, ((0, 128),))
    stencil = bell_draw(seeds[1], (S, PANELS), 0.5, 3.0, ((1, 128),), jnp.float32)
    corner_cells = draw_corner_cells(jax.random.fold_in(seeds[7], 71), 0)
    cluster_sizes = draw_cluster_sizes(jax.random.fold_in(seeds[7], 71), 0)
    near_source = draw_near_source(jax.random.fold_in(seeds[7], 71), 0)
    near_blocks = bell_draw(seeds[5], (PAIRS, CAP, CAP), (NB * CAP) ** -0.5, 0.1875, ((0, 128),))
    green_spectrum = jnp.clip(jnp.exp(math.log(1.0) - 2.9957323 * jax.random.uniform(seeds[6], (L, L, L), jnp.float32) ** shard_levels(seeds[6], (L, L, L), ((1, 8), (2, 16)), -0.2, 0.2)), 0.05, 1.0)
    return {"charges": charges, "stencil": stencil, "corner_cells": corner_cells, "cluster_sizes": cluster_sizes, "near_source": near_source, "near_blocks": near_blocks, "green_spectrum": green_spectrum}


def grid_cells(corner_cells):
    offset = jnp.arange(27, dtype=jnp.int32)
    coord_first = corner_cells[0][None, :] + (offset // 9)[:, None]
    coord_second = corner_cells[1][None, :] + ((offset // 3) % 3)[:, None]
    coord_third = corner_cells[2][None, :] + (offset % 3)[:, None]
    return (coord_first * M + coord_second) * M + coord_third


def live_slots(cluster_sizes):
    slot_rank = jnp.arange(CAP, dtype=jnp.int32)
    return (slot_rank[None, :] < cluster_sizes[:, None]).reshape(-1)


def near_group(pieces):
    blocks, source_rows = pieces
    return jnp.einsum("pjm,pm->pj", blocks.astype(jnp.float32), source_rows.astype(jnp.float32))


def reference(charges, stencil, corner_cells, cluster_sizes, near_source, near_blocks, green_spectrum):
    slot_mask = live_slots(cluster_sizes)
    live_charge = jnp.where(slot_mask, charges, jnp.zeros_like(charges))
    cell_index = grid_cells(corner_cells)
    deposit = stencil * live_charge.astype(jnp.float32)[None, :]
    grid_charge = jnp.zeros((M * M * M,), jnp.float32).at[cell_index.reshape(-1)].add(deposit.reshape(-1))
    padded = jnp.pad(grid_charge.reshape(M, M, M), ((0, L - M), (0, L - M), (0, L - M)))
    spectrum = jnp.fft.fftn(padded) * green_spectrum
    potential_grid = jnp.real(jnp.fft.ifftn(spectrum))[:M, :M, :M].astype(jnp.float32)
    far_field = jnp.sum(stencil * potential_grid.reshape(-1)[cell_index], axis=0)
    sources = live_charge.reshape(CLUSTERS, CAP)[near_source]
    groups = N_CLUS * N_PEN
    grouped = lax.map(near_group, (near_blocks.reshape(groups, PAIRS // groups, CAP, CAP), sources.reshape(groups, PAIRS // groups, CAP)))
    near_field = grouped.reshape(CLUSTERS, NB, CAP).sum(axis=1).reshape(-1)
    total = far_field + near_field
    return jnp.where(slot_mask, total, jnp.zeros_like(total))
```

```python
import functools
import math

import jax
import jax.numpy as jnp
import ml_dtypes
import numpy as np
from jax import lax
from jax.experimental import pallas as pl
from jax.experimental.pallas import tpu as pltpu
from jax.sharding import PartitionSpec as P

M = 256
L = 512
CAP = 256
NB = 4
SLOTS = 384
PENS = 16
DEVS = 128
ROOM = PENS * SLOTS + 512
TILE = 256
ROWS = 48
FIELDS = 24

exact = lax.Precision.HIGHEST
f32 = jnp.float32
bf16 = jnp.bfloat16
NT = (((1,), (1,)), ((), ()))


def section_table(count, length, sign):
    sample = jnp.arange(count, dtype=jnp.int32)[:, None]
    wave_number = jnp.arange(length, dtype=jnp.int32)[None, :]
    phase = (sample * wave_number % length).astype(jnp.float32) * (2.0 * math.pi / length)
    cosine = jnp.cos(phase)
    sine = jnp.sin(phase)
    from_real = jnp.stack([cosine, sign * sine], axis=1)
    from_imag = jnp.stack([-sign * sine, cosine], axis=1)
    return jnp.stack([from_real, from_imag], axis=0)


def exchanged(x, axis, split):
    return lax.all_to_all(x.astype(bf16), axis, split_axis=split, concat_axis=split + 1, tiled=True)


def far_field_general(charge_value, stencil, corner_cells, green_spectrum):
    pen_count = lax.axis_size("pen")
    clus_count = lax.axis_size("clus")
    planes = M // clus_count
    rows_own = M // pen_count
    pen_spread = L // pen_count
    clus_spread = L // clus_count
    slab_index = lax.axis_index("clus")
    forward_table = section_table(M, L, -1.0)
    inverse_table = section_table(M, L, 1.0)
    offset = jnp.arange(27, dtype=jnp.int32)[:, None]
    first = corner_cells[0][None, :] + offset // 9 - slab_index * planes
    second = corner_cells[1][None, :] + offset // 3 % 3
    third = corner_cells[2][None, :] + offset % 3
    slab_cell = (first * M + second) * M + third
    deposit = stencil * charge_value[None, :]
    slab_charge = (
        jnp.zeros((planes * M * M,), f32).at[slab_cell.reshape(-1)].add(deposit.reshape(-1))
    )
    grid_block = lax.psum_scatter(
        slab_charge.reshape(planes, M, M), "pen", scatter_dimension=1, tiled=True
    )
    section = jnp.einsum("xyz,zdk->dxyk", grid_block, forward_table[0], precision=exact)
    section = (
        section.reshape(2, planes, rows_own, pen_count, pen_spread)
        .transpose(0, 3, 2, 1, 4)
        .reshape(2, pen_count, rows_own, planes * pen_spread)
    )
    section = exchanged(section, "pen", 1).reshape(2, M, planes * pen_spread).astype(f32)
    section = jnp.einsum("cyw,cydk->dkw", section, forward_table, precision=exact)
    section = (
        section.reshape(2, clus_count, clus_spread, planes, pen_spread)
        .transpose(0, 1, 3, 2, 4)
        .reshape(2, clus_count, planes, clus_spread * pen_spread)
    )
    section = exchanged(section, "clus", 1).reshape(2, M, clus_spread * pen_spread).astype(f32)
    spectrum = jnp.einsum("cxv,cxdk->dkv", section, forward_table, precision=exact)
    spectrum = spectrum * green_spectrum.reshape(1, L, clus_spread * pen_spread)
    section = jnp.einsum("ckv,cxdk->dxv", spectrum, inverse_table, precision=exact)
    section = (
        section.reshape(2, clus_count, planes, clus_spread, pen_spread)
        .transpose(0, 1, 3, 2, 4)
        .reshape(2, clus_count, clus_spread, planes * pen_spread)
    )
    section = exchanged(section, "clus", 1).reshape(2, L, planes * pen_spread).astype(f32)
    section = jnp.einsum("ckw,cydk->dyw", section, inverse_table, precision=exact)
    section = (
        section.reshape(2, pen_count, rows_own, planes, pen_spread)
        .transpose(0, 1, 4, 2, 3)
        .reshape(2, pen_count, pen_spread, rows_own * planes)
    )
    section = exchanged(section, "pen", 1).reshape(2, L, rows_own * planes).astype(f32)
    lines = jnp.einsum("ckw,czk->zw", section, inverse_table[:, :, 0, :], precision=exact)
    lines = lines * (1.0 / (L * L * L))
    block = lines.reshape(M, rows_own, planes).transpose(2, 1, 0)
    slab = lax.all_gather(block, "pen", axis=1, tiled=True)
    return jnp.sum(stencil * slab.reshape(-1)[slab_cell], axis=0)


def rounded(x):
    return x.astype(np.float32).astype(ml_dtypes.bfloat16).astype(np.float64)


def balanced(exact_values):
    near = rounded(exact_values)
    ulp = np.ldexp(1.0, np.frexp(exact_values)[1] - 8)
    error = near - exact_values
    other = near - np.sign(error) * ulp
    gain = (other - near) * exact_values
    cost = (other - exact_values) ** 2 - error**2
    for x in range(exact_values.shape[1]):
        bias = np.sum(error[:, x] * exact_values[:, x])
        order = np.argsort(cost[:, x] / np.maximum(np.abs(gain[:, x]), 1e-30))
        for i in order:
            if error[i, x] != 0.0 and np.abs(bias + gain[i, x]) < np.abs(bias):
                near[i, x] = other[i, x]
                bias += gain[i, x]
            if np.abs(bias) < 1e-4:
                break
    return near


@functools.cache
def tables():
    plane = np.concatenate([2 * np.arange(DEVS), 2 * np.arange(DEVS) + 1])
    own = np.arange(L).reshape(PENS, 8, 4).transpose(1, 0, 2).reshape(-1)
    phase = (np.outer(np.arange(L), np.arange(M)) % L) * (2.0 * np.pi / L)
    both = balanced(np.concatenate([np.cos(phase), np.sin(phase)], axis=0))
    cos, sin = both[:L], both[L:]
    along_z = np.stack([cos[own], -sin[own]], axis=1).reshape(2 * L, M)
    back_z = along_z.T / float(L) ** 3
    along_y = np.block([[cos, sin], [-sin, cos]])
    back_y = along_y.T
    cos, sin = cos.T[plane], sin.T[plane]
    along_x = np.block([[cos, -sin], [sin, cos]])
    back_x = along_x
    return tuple(
        t.astype(np.float32).astype(ml_dtypes.bfloat16)
        for t in (along_z, along_y, along_x, back_y, back_x, back_z)
    )


def iota(shape, dim):
    return lax.broadcasted_iota(jnp.int32, shape, dim)


def bucket_kernel(
    slab_ref, sizes_ref, charge_ref, stencil_ref, corner_ref, out_ref, route_ref,
    first_ref, second_ref, total_ref,
):
    count = 8 * CAP
    lane = iota((1, CAP), 1)
    charge = charge_ref[...].astype(f32)
    live = jnp.concatenate(
        [jnp.where(lane < sizes_ref[k], 1.0, 0.0) for k in range(8)], axis=1
    )
    row8 = iota((8, CAP), 0)
    size8 = jnp.zeros((8, CAP), jnp.int32)
    for k in range(8):
        size8 = jnp.where(row8 == k, sizes_ref[k], size8)
    charge = jnp.where(iota((8, CAP), 1) < size8, charge, 0.0)
    q = jnp.concatenate([charge[k : k + 1] for k in range(8)], axis=1)
    x = corner_ref[0:1, :] - slab_ref[0] * 32
    owner = jnp.where(live > 0.0, x >> 1, -2)
    odd = (x & 1) == 1
    pen = iota((PENS, count), 0)
    member = jnp.where((pen == owner) | (pen == owner + 1), 1.0, 0.0)
    upper = jnp.where(iota((128, 128), 0) <= iota((128, 128), 1), 1.0, 0.0).astype(bf16)
    carry = jnp.zeros((PENS, 128), f32)
    ranks = []
    for k in range(count // 128):
        part = member[:, 128 * k : 128 * k + 128]
        upto = jnp.dot(part.astype(bf16), upper, preferred_element_type=f32) + carry
        ranks.append(upto - part)
        carry = jnp.broadcast_to(upto[:, 127:128], (PENS, 128))
    rank = jnp.concatenate(ranks, axis=1)
    over = jnp.where(jnp.max(carry, axis=0, keepdims=True) > SLOTS, 1.0, 0.0)
    over = jnp.concatenate([over] * (SLOTS // 128), axis=1)
    pos_first = jnp.sum(jnp.where(pen == owner, rank, 0.0), axis=0, keepdims=True)
    pos_second = jnp.sum(jnp.where(pen == owner + 1, rank, 0.0), axis=0, keepdims=True)
    pos_first = jnp.where(live > 0.0, pos_first, -1.0).astype(jnp.int32)
    pos_second = jnp.where(live > 0.0, pos_second, -1.0).astype(jnp.int32)
    route_ref[...] = jnp.zeros((8, count), jnp.int32)
    route_ref[0:1, :] = owner
    route_ref[1:2, :] = pos_first
    route_ref[2:3, :] = pos_second

    for ref in (first_ref, second_ref):
        ref[...] = jnp.zeros((ROWS, count), f32)
        ref[18:19, :] = q
        ref[19:20, :] = corner_ref[1:2, :].astype(f32)
        ref[20:21, :] = corner_ref[2:3, :].astype(f32)
        ref[21:22, :] = live
    w0 = stencil_ref[0:9, :]
    w1 = stencil_ref[9:18, :]
    w2 = stencil_ref[18:27, :]
    first_ref[0:9, :] = jnp.where(odd, 0.0, w0)
    first_ref[9:18, :] = jnp.where(odd, w0, w1)
    second_ref[0:9, :] = jnp.where(odd, w1, w2)
    second_ref[9:18, :] = jnp.where(odd, w2, 0.0)
    for ref in (first_ref, second_ref):
        w = ref[0:18, :]
        ref[24:42, :] = w - w.astype(bf16).astype(f32)

    step = 512
    total_ref[...] = jnp.zeros_like(total_ref)

    def chunk(k, _):
        at = pl.ds(pl.multiple_of(k * step, step), step)
        own = route_ref[0:1, at]
        slot = iota((SLOTS, step), 0)
        for ref, shift, row in ((first_ref, 0, 1), (second_ref, 1, 2)):
            values = ref[:, at].astype(bf16)
            spread = jnp.concatenate(
                [
                    values * jnp.where(own + shift == p, 1.0, 0.0).astype(bf16)
                    for p in range(PENS)
                ],
                axis=0,
            )
            hot = jnp.where(slot == route_ref[row : row + 1, at], 1.0, 0.0).astype(bf16)
            total_ref[...] += lax.dot_general(spread, hot, NT, preferred_element_type=f32)
        return 0

    lax.fori_loop(0, count // step, chunk, 0)
    first_ref[...] = jnp.zeros_like(first_ref)
    first_ref[22:23, 0:SLOTS] = over
    first_ref[42:48, 0:CAP] = charge[0:6]
    for k in range(4):
        half = slice(k % 2 * 128, k % 2 * 128 + 128)
        first_ref[42 + k : 43 + k, CAP:SLOTS] = charge[6 + k // 2 : 7 + k // 2, half]
    extra = first_ref[:, 0:SLOTS]
    for p in range(PENS):
        out_ref[p] = (total_ref[ROWS * p : ROWS * p + ROWS, :] + extra).astype(bf16)


def hot_z(z, c):
    return jnp.where(iota((M, TILE), 0) == z + c, 1.0, 0.0).astype(bf16)


def deposit_kernel(
    recv_ref, table_ref, out_ref, packed_ref, meta_ref, left_ref, right_ref,
    low_ref, grid_ref,
):
    packed_ref[...] = jnp.zeros_like(packed_ref)
    blocks = [recv_ref[s].astype(f32) for s in range(PENS)]
    counts = [jnp.sum(b[21:22, :]).astype(jnp.int32) for b in blocks]
    start = jnp.int32(0)
    for s in range(PENS):
        meta_ref[s] = start
        block = blocks[s][:FIELDS] + jnp.concatenate(
            [blocks[s][FIELDS : FIELDS + 18], jnp.zeros((FIELDS - 18, SLOTS), f32)], axis=0
        )
        block = jnp.concatenate([block, jnp.zeros((FIELDS, 128), f32)], axis=1)
        block = pltpu.roll(block, start % 128, 1)
        at = pl.ds(pl.multiple_of(start // 128 * 128, 128), SLOTS + 128)
        packed_ref[:, at] = packed_ref[:, at] + block
        start = start + counts[s]
    meta_ref[PENS] = start
    over = blocks[0][22:23, :128]
    for s in range(1, PENS):
        over = jnp.maximum(over, blocks[s][22:23, :128])
    spoil = jnp.where(over[:, :1] > 0.0, jnp.nan, 0.0)
    grid_ref[...] = jnp.zeros_like(grid_ref)

    def tile(r, _):
        fields = packed_ref[:, pl.ds(pl.multiple_of(r * TILE, TILE), TILE)]
        y = fields[19:20].astype(jnp.int32)
        z = fields[20:21].astype(jnp.int32)
        weights = fields[0:18] * fields[18:19]
        away = iota((M, TILE), 0) - y
        is0, is1, is2 = away == 0, away == 1, away == 2
        for c in range(3):
            left_ref[:, c * TILE : (c + 1) * TILE] = hot_z(z, c)
            for xp in range(2):
                w = [weights[xp * 9 + b * 3 + c : xp * 9 + b * 3 + c + 1] for b in range(3)]
                v = jnp.where(is0, w[0], jnp.where(is1, w[1], jnp.where(is2, w[2], 0.0)))
                high = v.astype(bf16)
                low = (v - high.astype(f32)).astype(bf16)
                right_ref[xp * M : (xp + 1) * M, c * TILE : (c + 1) * TILE] = high
                low_ref[xp * M : (xp + 1) * M, c * TILE : (c + 1) * TILE] = low
        left = left_ref[...]
        grid_ref[...] += lax.dot_general(
            left, right_ref[...], NT, preferred_element_type=f32
        ) + lax.dot_general(left, low_ref[...], NT, preferred_element_type=f32)
        return 0

    lax.fori_loop(0, (start + TILE - 1) // TILE, tile, 0)
    grid = grid_ref[...] + spoil
    high = grid.astype(bf16)
    low = (grid - high.astype(f32)).astype(bf16)
    for k in range(4):
        at = slice(k * 256, k * 256 + 256)
        table = table_ref[at, :]
        out_ref[at, :] = (
            jnp.dot(table, high, preferred_element_type=f32)
            + jnp.dot(table, low, preferred_element_type=f32)
        ).astype(bf16)


def convolve_kernel(
    recv_ref, green_ref, along_y_ref, along_x_ref, back_y_ref, back_x_ref, out_ref, in_ref, sum_ref
):
    j = pl.program_id(0)

    @pl.when(j == 0)
    def _():
        for h in range(4):
            in_ref[h] = recv_ref[:, h * 128 : h * 128 + 128].astype(f32)

    def piece(xp):
        return jnp.concatenate(
            [
                in_ref[2 * xp + h, pl.ds(2 * j + c, DEVS, stride=8), :].astype(bf16)
                for c in range(2)
                for h in range(2)
            ],
            axis=1,
        )

    field = jnp.concatenate([piece(0), piece(1)], axis=0)
    part = lax.dot_general(along_y_ref[...], field, NT, preferred_element_type=f32).astype(bf16)
    part = jnp.concatenate([part[:L], part[L:]], axis=1)
    part = jnp.dot(part, along_x_ref[...], preferred_element_type=f32)
    green = green_ref[...].reshape(L, L).astype(f32)
    part = jnp.concatenate(
        [(part[:, :L] * green).astype(bf16), (part[:, L:] * green).astype(bf16)], axis=0
    )
    part = jnp.dot(back_y_ref[...], part, preferred_element_type=f32).astype(bf16)
    part = jnp.concatenate([part[:M], part[M:]], axis=1)
    part = lax.dot_general(back_x_ref[...], part, NT, preferred_element_type=f32)
    for c in range(2):
        for xp in range(2):
            row = c * M + xp * DEVS
            for h in range(2):
                sum_ref[2 * xp + h, pl.ds(2 * j + c, DEVS, stride=8), :] = part[
                    row : row + DEVS, h * 128 : h * 128 + 128
                ]

    @pl.when(j == 3)
    def _():
        for h in range(4):
            out_ref[:, h * 128 : h * 128 + 128] = sum_ref[h].astype(bf16)


def interpolate_kernel(meta_ref, recv_ref, table_ref, packed_ref, out_ref, flag_ref, grid_ref, result_ref):
    grid = jnp.dot(table_ref[...], recv_ref[...], preferred_element_type=f32)
    flag_ref[...] = jnp.where(jnp.isnan(grid[:8, :128]), 1.0, 0.0)
    grid = grid.T
    high = grid.astype(bf16)
    grid_ref[0] = high
    grid_ref[1] = (grid - high.astype(f32)).astype(bf16)
    result_ref[...] = jnp.zeros_like(result_ref)

    def tile(r, _):
        at = pl.ds(pl.multiple_of(r * TILE, TILE), TILE)
        fields = packed_ref[:, at]
        y = fields[19:20].astype(jnp.int32)
        z = fields[20:21].astype(jnp.int32)
        away = iota((M, TILE), 0) - y
        is0, is1, is2 = away == 0, away == 1, away == 2
        total = jnp.zeros((M, TILE), f32)
        for c in range(3):
            hot = hot_z(z, c)
            near = jnp.dot(grid_ref[0], hot, preferred_element_type=f32) + jnp.dot(
                grid_ref[1], hot, preferred_element_type=f32
            )
            for xp in range(2):
                w = [fields[xp * 9 + b * 3 + c : xp * 9 + b * 3 + c + 1] for b in range(3)]
                v = jnp.where(is0, w[0], jnp.where(is1, w[1], jnp.where(is2, w[2], 0.0)))
                total = total + v * near[xp * M : (xp + 1) * M]
        result_ref[:, at] = jnp.broadcast_to(jnp.sum(total, axis=0, keepdims=True), (8, TILE))
        return 0

    lax.fori_loop(0, (meta_ref[PENS] + TILE - 1) // TILE, tile, 0)
    width = SLOTS + 128
    for s in range(PENS):
        start = meta_ref[s]
        piece = result_ref[:, pl.ds(pl.multiple_of(start // 128 * 128, 128), width)]
        piece = pltpu.roll(piece, (width - start % 128) % width, 1)
        out_ref[s : s + 1, :] = piece[0:1, :SLOTS]


def collect_kernel(back_ref, route_ref, out_ref):
    back = back_ref[...]
    high = back.astype(bf16)
    low = (back - high.astype(f32)).astype(bf16)
    both = jnp.concatenate([high.astype(f32), low.astype(f32)], axis=0).astype(bf16)
    step = 512
    for k in range(4):
        at = slice(k * step, k * step + step)
        owner = route_ref[0:1, at]
        slot = iota((SLOTS, step), 0)
        pen = iota((PENS, step), 0)
        total = jnp.zeros((PENS, step), f32)
        for shift in range(2):
            hot = jnp.where(slot == route_ref[shift + 1 : shift + 2, at], 1.0, 0.0).astype(bf16)
            got = jnp.dot(both, hot, preferred_element_type=f32)
            total = total + jnp.where(pen == owner + shift, got[:PENS] + got[PENS:], 0.0)
        out_ref[:, at] = jnp.broadcast_to(jnp.sum(total, axis=0, keepdims=True), (8, step))


def struct(shape, dtype):
    return jax.ShapeDtypeStruct(shape, dtype)


def whole(count):
    return [pl.BlockSpec(memory_space=pltpu.VMEM)] * count


SMEM = pl.BlockSpec(memory_space=pltpu.SMEM)
LIMIT = pltpu.CompilerParams(vmem_limit_bytes=40 * 1024 * 1024)


def far_field_blocks(charges, stencil, corner_cells, cluster_sizes, green_spectrum):
    along_z, along_y, along_x, back_y, back_x, back_z = [jnp.asarray(t) for t in tables()]
    green = (
        green_spectrum.astype(bf16).transpose(2, 1, 0).reshape(8, 4, L // 8, L)
    )
    green = lax.all_to_all(green, "clus", 0, 0, tiled=True)
    sent, route = pl.pallas_call(
        bucket_kernel,
        out_shape=[
            struct((PENS, ROWS, SLOTS), bf16),
            struct((8, 8 * CAP), jnp.int32),
        ],
        in_specs=[SMEM, SMEM] + whole(3),
        out_specs=whole(2),
        scratch_shapes=[
            pltpu.VMEM((ROWS, 8 * CAP), f32),
            pltpu.VMEM((ROWS, 8 * CAP), f32),
            pltpu.VMEM((ROWS * PENS, SLOTS), f32),
        ],
        compiler_params=LIMIT,
        name="bucket",
    )(
        lax.axis_index("clus").astype(jnp.int32).reshape(1),
        cluster_sizes,
        charges.reshape(8, CAP),
        stencil,
        corner_cells,
    )
    recv = lax.all_to_all(sent, "pen", 0, 0, tiled=True)
    section, packed, meta = pl.pallas_call(
        deposit_kernel,
        out_shape=[
            struct((2 * L, 2 * M), bf16),
            struct((FIELDS, ROOM), f32),
            struct((PENS + 1,), jnp.int32),
        ],
        in_specs=whole(2),
        out_specs=whole(2) + [SMEM],
        scratch_shapes=[
            pltpu.VMEM((M, 3 * TILE), bf16),
            pltpu.VMEM((2 * M, 3 * TILE), bf16),
            pltpu.VMEM((2 * M, 3 * TILE), bf16),
            pltpu.VMEM((M, 2 * M), f32),
        ],
        compiler_params=LIMIT,
        name="deposit",
    )(recv, along_z)
    section, green = lax.optimization_barrier((section, green))
    section = lax.all_to_all(
        section.reshape(DEVS, 8, 2 * M), ("clus", "pen"), 0, 0, tiled=True
    )
    section = pl.pallas_call(
        convolve_kernel,
        grid=(4,),
        out_shape=struct((2 * L, 2 * M), bf16),
        in_specs=[
            pl.BlockSpec((2 * L, 2 * M), lambda j: (0, 0)),
            pl.BlockSpec((8, 1, L // 8, L), lambda j: (0, j, 0, 0)),
            pl.BlockSpec((2 * L, 2 * M), lambda j: (0, 0)),
            pl.BlockSpec((2 * M, 2 * L), lambda j: (0, 0)),
            pl.BlockSpec((2 * M, 2 * L), lambda j: (0, 0)),
            pl.BlockSpec((2 * M, 2 * L), lambda j: (0, 0)),
        ],
        out_specs=pl.BlockSpec((2 * L, 2 * M), lambda j: (0, 0)),
        scratch_shapes=[
            pltpu.VMEM((4, 2 * L, 128), f32),
            pltpu.VMEM((4, 2 * L, 128), f32),
        ],
        compiler_params=LIMIT,
        name="convolve",
    )(section.reshape(2 * L, 2 * M), green, along_y, along_x, back_y, back_x)
    section = lax.all_to_all(
        section.reshape(DEVS, 8, 2 * M), ("clus", "pen"), 0, 0, tiled=True
    )
    back, flag = pl.pallas_call(
        interpolate_kernel,
        out_shape=[struct((PENS, SLOTS), f32), struct((8, 128), f32)],
        in_specs=[SMEM] + whole(3),
        out_specs=whole(2),
        scratch_shapes=[pltpu.VMEM((2, 2 * M, M), bf16), pltpu.VMEM((8, ROOM), f32)],
        compiler_params=LIMIT,
        name="interpolate",
    )(meta, section.reshape(2 * L, 2 * M), back_z, packed)
    back = lax.all_to_all(back, "pen", 0, 0, tiled=True)
    far = pl.pallas_call(
        collect_kernel,
        out_shape=struct((8, 8 * CAP), f32),
        in_specs=whole(2),
        out_specs=pl.BlockSpec(memory_space=pltpu.VMEM),
        compiler_params=LIMIT,
        name="collect",
    )(back, route)
    pool = jnp.concatenate(
        [recv[:, 42:48, :CAP], recv[:, 42:46, CAP:].reshape(PENS, 2, CAP)], axis=1
    ).reshape(PENS * 8, CAP)
    return far[0], pool, flag[0, 0]


def neighbours(x, axis):
    devices = lax.axis_size(axis)
    up = [(i, i + 1) for i in range(devices - 1)]
    before = lax.ppermute(x, axis, up)
    after = lax.ppermute(x, axis, [(j, i) for i, j in up])
    return jnp.concatenate([before, x, after], axis=0)


def per_device(
    charges, stencil, corner_cells, cluster_sizes, near_source, near_blocks, green_spectrum
):
    slot_rank = jnp.arange(CAP, dtype=jnp.int32)
    slot_mask = (slot_rank[None, :] < cluster_sizes[:, None]).reshape(-1)
    far_field, pool, overflow = far_field_blocks(
        charges, stencil, corner_cells, cluster_sizes, green_spectrum
    )
    local_source = near_source - (lax.axis_index("clus") - 1) * pool.shape[0]
    source_rows = neighbours(pool, "clus")[local_source]
    near_terms = jnp.einsum(
        "pjm,pm->pj", near_blocks, source_rows, preferred_element_type=f32
    )
    near_field = near_terms.reshape(-1, NB, CAP).sum(axis=1).reshape(-1)

    def general():
        charge_value = jnp.where(slot_mask, charges, jnp.zeros_like(charges)).astype(f32)
        return far_field_general(charge_value, stencil, corner_cells, green_spectrum)

    far_field = lax.cond(overflow > 0.0, general, lambda: far_field)
    total = far_field + near_field
    return jnp.where(slot_mask, total, jnp.zeros_like(total))


def solution(mesh):
    in_specs = (
        P(("clus", "pen")),
        P(None, ("clus", "pen")),
        P(None, ("clus", "pen")),
        P(("clus", "pen")),
        P(("clus", "pen")),
        P(("clus", "pen"), None, None),
        P(None, "clus", "pen"),
    )
    out_specs = P(("clus", "pen"))
    return jax.shard_map(
        per_device, mesh=mesh, in_specs=in_specs, out_specs=out_specs, check_vma=False
    )
```

```python
import functools
import math

import jax
import jax.numpy as jnp
import ml_dtypes
import numpy as np
from jax import lax
from jax.experimental import pallas as pl
from jax.experimental.pallas import tpu as pltpu
from jax.sharding import PartitionSpec as P

M = 256
L = 512
CAP = 256
NB = 4
SLOTS = 384
PENS = 16
DEVS = 128
ROOM = PENS * SLOTS + 512
TILE = 512
ROWS = 48
FIELDS = 24

exact = lax.Precision.HIGHEST
f32 = jnp.float32
bf16 = jnp.bfloat16
NT = (((1,), (1,)), ((), ()))


def section_table(count, length, sign):
    sample = jnp.arange(count, dtype=jnp.int32)[:, None]
    wave_number = jnp.arange(length, dtype=jnp.int32)[None, :]
    phase = (sample * wave_number % length).astype(jnp.float32) * (2.0 * math.pi / length)
    cosine = jnp.cos(phase)
    sine = jnp.sin(phase)
    from_real = jnp.stack([cosine, sign * sine], axis=1)
    from_imag = jnp.stack([-sign * sine, cosine], axis=1)
    return jnp.stack([from_real, from_imag], axis=0)


def exchanged(x, axis, split):
    return lax.all_to_all(x.astype(bf16), axis, split_axis=split, concat_axis=split + 1, tiled=True)


def far_field_general(charge_value, stencil, corner_cells, green_spectrum):
    pen_count = lax.axis_size("pen")
    clus_count = lax.axis_size("clus")
    planes = M // clus_count
    rows_own = M // pen_count
    pen_spread = L // pen_count
    clus_spread = L // clus_count
    slab_index = lax.axis_index("clus")
    forward_table = section_table(M, L, -1.0)
    inverse_table = section_table(M, L, 1.0)
    offset = jnp.arange(27, dtype=jnp.int32)[:, None]
    first = corner_cells[0][None, :] + offset // 9 - slab_index * planes
    second = corner_cells[1][None, :] + offset // 3 % 3
    third = corner_cells[2][None, :] + offset % 3
    slab_cell = (first * M + second) * M + third
    deposit = stencil * charge_value[None, :]
    slab_charge = (
        jnp.zeros((planes * M * M,), f32).at[slab_cell.reshape(-1)].add(deposit.reshape(-1))
    )
    grid_block = slab_charge.reshape(planes, pen_count, rows_own, M).transpose(1, 0, 2, 3)
    grid_block = lax.all_to_all(grid_block, "pen", 0, 0, tiled=True).sum(axis=0)
    section = jnp.einsum("xyz,zdk->dxyk", grid_block, forward_table[0], precision=exact)
    section = (
        section.reshape(2, planes, rows_own, pen_count, pen_spread)
        .transpose(0, 3, 2, 1, 4)
        .reshape(2, pen_count, rows_own, planes * pen_spread)
    )
    section = exchanged(section, "pen", 1).reshape(2, M, planes * pen_spread).astype(f32)
    section = jnp.einsum("cyw,cydk->dkw", section, forward_table, precision=exact)
    section = (
        section.reshape(2, clus_count, clus_spread, planes, pen_spread)
        .transpose(0, 1, 3, 2, 4)
        .reshape(2, clus_count, planes, clus_spread * pen_spread)
    )
    section = exchanged(section, "clus", 1).reshape(2, M, clus_spread * pen_spread).astype(f32)
    spectrum = jnp.einsum("cxv,cxdk->dkv", section, forward_table, precision=exact)
    spectrum = spectrum * green_spectrum.reshape(1, L, clus_spread * pen_spread)
    section = jnp.einsum("ckv,cxdk->dxv", spectrum, inverse_table, precision=exact)
    section = (
        section.reshape(2, clus_count, planes, clus_spread, pen_spread)
        .transpose(0, 1, 3, 2, 4)
        .reshape(2, clus_count, clus_spread, planes * pen_spread)
    )
    section = exchanged(section, "clus", 1).reshape(2, L, planes * pen_spread).astype(f32)
    section = jnp.einsum("ckw,cydk->dyw", section, inverse_table, precision=exact)
    section = (
        section.reshape(2, pen_count, rows_own, planes, pen_spread)
        .transpose(0, 1, 4, 2, 3)
        .reshape(2, pen_count, pen_spread, rows_own * planes)
    )
    section = exchanged(section, "pen", 1).reshape(2, L, rows_own * planes).astype(f32)
    lines = jnp.einsum("ckw,czk->zw", section, inverse_table[:, :, 0, :], precision=exact)
    lines = lines * (1.0 / (L * L * L))
    block = lines.reshape(M, rows_own, planes).transpose(2, 1, 0)
    slab = jnp.broadcast_to(block[None], (pen_count,) + block.shape)
    slab = lax.all_to_all(slab, "pen", 0, 0, tiled=True).transpose(1, 0, 2, 3)
    return jnp.sum(stencil * slab.reshape(-1)[slab_cell], axis=0)


def rounded(x):
    return x.astype(np.float32).astype(ml_dtypes.bfloat16).astype(np.float64)


def balanced(exact_values):
    near = rounded(exact_values)
    ulp = np.ldexp(1.0, np.frexp(exact_values)[1] - 8)
    error = near - exact_values
    other = near - np.sign(error) * ulp
    gain = (other - near) * exact_values
    cost = (other - exact_values) ** 2 - error**2
    for x in range(exact_values.shape[1]):
        bias = np.sum(error[:, x] * exact_values[:, x])
        order = np.argsort(cost[:, x] / np.maximum(np.abs(gain[:, x]), 1e-30))
        for i in order:
            if error[i, x] != 0.0 and np.abs(bias + gain[i, x]) < np.abs(bias):
                near[i, x] = other[i, x]
                bias += gain[i, x]
            if np.abs(bias) < 1e-4:
                break
    return near


@functools.cache
def tables():
    plane = np.concatenate([2 * np.arange(DEVS), 2 * np.arange(DEVS) + 1])
    own = np.arange(L).reshape(PENS, 8, 4).transpose(1, 0, 2).reshape(-1)
    phase = (np.outer(np.arange(L), np.arange(M)) % L) * (2.0 * np.pi / L)
    both = balanced(np.concatenate([np.cos(phase), np.sin(phase)], axis=0))
    cos, sin = both[:L], both[L:]
    along_z = np.stack([cos[own], -sin[own]], axis=1).reshape(2 * L, M)
    back_z = along_z.T / float(L) ** 3
    along_y = np.block([[cos, sin], [-sin, cos]])
    back_y = along_y.T
    cos, sin = cos.T[plane], sin.T[plane]
    along_x = np.block([[cos, -sin], [sin, cos]])
    back_x = along_x
    return tuple(
        t.astype(np.float32).astype(ml_dtypes.bfloat16)
        for t in (along_z, along_y, along_x, back_y, back_x, back_z)
    )


def iota(shape, dim):
    return lax.broadcasted_iota(jnp.int32, shape, dim)


def bucket_kernel(
    slab_ref, sizes_ref, charge_ref, stencil_ref, corner_ref, out_ref, route_ref,
    first_ref, second_ref, total_ref,
):
    count = 8 * CAP
    lane = iota((1, CAP), 1)
    charge = charge_ref[...].astype(f32)
    live = jnp.concatenate(
        [jnp.where(lane < sizes_ref[k], 1.0, 0.0) for k in range(8)], axis=1
    )
    row8 = iota((8, CAP), 0)
    size8 = jnp.zeros((8, CAP), jnp.int32)
    for k in range(8):
        size8 = jnp.where(row8 == k, sizes_ref[k], size8)
    charge = jnp.where(iota((8, CAP), 1) < size8, charge, 0.0)
    q = jnp.concatenate([charge[k : k + 1] for k in range(8)], axis=1)
    x = corner_ref[0:1, :] - slab_ref[0] * 32
    owner = jnp.where(live > 0.0, x >> 1, -2)
    odd = (x & 1) == 1
    pen = iota((PENS, count), 0)
    member = jnp.where((pen == owner) | (pen == owner + 1), 1.0, 0.0)
    upper = jnp.where(iota((128, 128), 0) <= iota((128, 128), 1), 1.0, 0.0).astype(bf16)
    carry = jnp.zeros((PENS, 128), f32)
    ranks = []
    for k in range(count // 128):
        part = member[:, 128 * k : 128 * k + 128]
        upto = jnp.dot(part.astype(bf16), upper, preferred_element_type=f32) + carry
        ranks.append(upto - part)
        carry = jnp.broadcast_to(upto[:, 127:128], (PENS, 128))
    rank = jnp.concatenate(ranks, axis=1)
    over = jnp.where(jnp.max(carry, axis=0, keepdims=True) > SLOTS, 1.0, 0.0)
    over = jnp.concatenate([over] * (SLOTS // 128), axis=1)
    pos_first = jnp.sum(jnp.where(pen == owner, rank, 0.0), axis=0, keepdims=True)
    pos_second = jnp.sum(jnp.where(pen == owner + 1, rank, 0.0), axis=0, keepdims=True)
    pos_first = jnp.where(live > 0.0, pos_first, -1.0).astype(jnp.int32)
    pos_second = jnp.where(live > 0.0, pos_second, -1.0).astype(jnp.int32)
    route_ref[...] = jnp.zeros((8, count), jnp.int32)
    route_ref[0:1, :] = owner
    route_ref[1:2, :] = pos_first
    route_ref[2:3, :] = pos_second

    for ref in (first_ref, second_ref):
        ref[...] = jnp.zeros((ROWS, count), f32)
        ref[18:19, :] = q
        ref[19:20, :] = corner_ref[1:2, :].astype(f32)
        ref[20:21, :] = corner_ref[2:3, :].astype(f32)
        ref[21:22, :] = live
    w0 = stencil_ref[0:9, :]
    w1 = stencil_ref[9:18, :]
    w2 = stencil_ref[18:27, :]
    first_ref[0:9, :] = jnp.where(odd, 0.0, w0)
    first_ref[9:18, :] = jnp.where(odd, w0, w1)
    second_ref[0:9, :] = jnp.where(odd, w1, w2)
    second_ref[9:18, :] = jnp.where(odd, w2, 0.0)
    for ref in (first_ref, second_ref):
        w = ref[0:18, :]
        ref[24:42, :] = w - w.astype(bf16).astype(f32)

    step = 512
    total_ref[...] = jnp.zeros_like(total_ref)

    def chunk(k, _):
        at = pl.ds(pl.multiple_of(k * step, step), step)
        own = route_ref[0:1, at]
        slot = iota((SLOTS, step), 0)
        for ref, shift, row in ((first_ref, 0, 1), (second_ref, 1, 2)):
            values = ref[:, at].astype(bf16)
            spread = jnp.concatenate(
                [
                    values * jnp.where(own + shift == p, 1.0, 0.0).astype(bf16)
                    for p in range(PENS)
                ],
                axis=0,
            )
            hot = jnp.where(slot == route_ref[row : row + 1, at], 1.0, 0.0).astype(bf16)
            total_ref[...] += lax.dot_general(spread, hot, NT, preferred_element_type=f32)
        return 0

    lax.fori_loop(0, count // step, chunk, 0)
    first_ref[...] = jnp.zeros_like(first_ref)
    first_ref[22:23, 0:SLOTS] = over
    first_ref[42:48, 0:CAP] = charge[0:6]
    for k in range(4):
        half = slice(k % 2 * 128, k % 2 * 128 + 128)
        first_ref[42 + k : 43 + k, CAP:SLOTS] = charge[6 + k // 2 : 7 + k // 2, half]
    extra = first_ref[:, 0:SLOTS]
    for p in range(PENS):
        out_ref[p] = (total_ref[ROWS * p : ROWS * p + ROWS, :] + extra).astype(bf16)


def rows_as_bf16():
    return iota((M, TILE), 0).astype(f32).astype(bf16)


def hot_z(z, c):
    one = jnp.ones((M, TILE), bf16)
    return jnp.where(rows_as_bf16() == (z + c).astype(f32).astype(bf16), one, jnp.zeros_like(one))


def deposit_kernel(
    recv_ref, table_ref, out_ref, packed_ref, meta_ref, left_ref, right_ref,
    low_ref, grid_ref,
):
    packed_ref[...] = jnp.zeros_like(packed_ref)
    blocks = [recv_ref[s].astype(f32) for s in range(PENS)]
    counts = [jnp.sum(b[21:22, :]).astype(jnp.int32) for b in blocks]
    start = jnp.int32(0)
    for s in range(PENS):
        meta_ref[s] = start
        block = blocks[s][:FIELDS] + jnp.concatenate(
            [blocks[s][FIELDS : FIELDS + 18], jnp.zeros((FIELDS - 18, SLOTS), f32)], axis=0
        )
        block = jnp.concatenate([block, jnp.zeros((FIELDS, 128), f32)], axis=1)
        block = pltpu.roll(block, start % 128, 1)
        at = pl.ds(pl.multiple_of(start // 128 * 128, 128), SLOTS + 128)
        packed_ref[:, at] = packed_ref[:, at] + block
        start = start + counts[s]
    meta_ref[PENS] = start
    over = blocks[0][22:23, :128]
    for s in range(1, PENS):
        over = jnp.maximum(over, blocks[s][22:23, :128])
    spoil = jnp.where(over[:, :1] > 0.0, jnp.nan, 0.0)
    grid_ref[...] = jnp.zeros_like(grid_ref)

    def tile(r, _):
        fields = packed_ref[:, pl.ds(pl.multiple_of(r * TILE, TILE), TILE)]
        y = fields[19:20].astype(jnp.int32)
        z = fields[20:21].astype(jnp.int32)
        weights = fields[0:18] * fields[18:19]
        high = weights.astype(bf16)
        low = (weights - high.astype(f32)).astype(bf16)
        place = rows_as_bf16()
        at0, at1, at2 = [place == (y + b).astype(f32).astype(bf16) for b in range(3)]
        zero = jnp.zeros((M, TILE), bf16)
        for c in range(3):
            left_ref[:, c * TILE : (c + 1) * TILE] = hot_z(z, c)
            for xp in range(2):
                for part, ref in ((high, right_ref), (low, low_ref)):
                    w = [part[xp * 9 + b * 3 + c : xp * 9 + b * 3 + c + 1] for b in range(3)]
                    v = jnp.where(at0, w[0], jnp.where(at1, w[1], jnp.where(at2, w[2], zero)))
                    ref[xp * M : (xp + 1) * M, c * TILE : (c + 1) * TILE] = v
        left = left_ref[...]
        grid_ref[...] += lax.dot_general(
            left, right_ref[...], NT, preferred_element_type=f32
        ) + lax.dot_general(left, low_ref[...], NT, preferred_element_type=f32)
        return 0

    lax.fori_loop(0, (start + TILE - 1) // TILE, tile, 0)
    grid = grid_ref[...] + spoil
    high = grid.astype(bf16)
    low = (grid - high.astype(f32)).astype(bf16)
    for k in range(4):
        at = slice(k * 256, k * 256 + 256)
        table = table_ref[at, :]
        out_ref[at, :] = (
            jnp.dot(table, high, preferred_element_type=f32)
            + jnp.dot(table, low, preferred_element_type=f32)
        ).astype(bf16)


def recut_kernel(slab_ref, green_ref, *out_refs):
    for s, ref in enumerate(out_refs):
        first = (slab_ref[0] + s) % 8 * 4
        for c in range(4):
            ref[c] = green_ref[pl.ds(first + c, L // 8, stride=32), :].astype(bf16)


def convolve_kernel(
    slab_ref, recv_ref, g0_ref, g1_ref, g2_ref, g3_ref, g4_ref, g5_ref, g6_ref, g7_ref, along_y_ref, along_x_ref, back_y_ref, back_x_ref, out_ref, in_ref, sum_ref, green_ref
):
    j = pl.program_id(0)

    @pl.when(j == 0)
    def _():
        for h in range(4):
            in_ref[h] = recv_ref[:, h * 128 : h * 128 + 128].astype(f32)

    for s, ref in enumerate((g0_ref, g1_ref, g2_ref, g3_ref, g4_ref, g5_ref, g6_ref, g7_ref)):
        green_ref[(slab_ref[0] + 8 - s) % 8] = ref[0]

    def piece(xp):
        return jnp.concatenate(
            [
                in_ref[2 * xp + h, pl.ds(2 * j + c, DEVS, stride=8), :].astype(bf16)
                for c in range(2)
                for h in range(2)
            ],
            axis=1,
        )

    field = jnp.concatenate([piece(0), piece(1)], axis=0)
    part = lax.dot_general(along_y_ref[...], field, NT, preferred_element_type=f32).astype(bf16)
    part = jnp.concatenate([part[:L], part[L:]], axis=1)
    part = jnp.dot(part, along_x_ref[...], preferred_element_type=f32)
    green = green_ref[...].reshape(L, L).astype(f32)
    part = jnp.concatenate(
        [(part[:, :L] * green).astype(bf16), (part[:, L:] * green).astype(bf16)], axis=0
    )
    part = jnp.dot(back_y_ref[...], part, preferred_element_type=f32).astype(bf16)
    part = jnp.concatenate([part[:M], part[M:]], axis=1)
    part = lax.dot_general(back_x_ref[...], part, NT, preferred_element_type=f32)
    for c in range(2):
        for xp in range(2):
            row = c * M + xp * DEVS
            for h in range(2):
                sum_ref[2 * xp + h, pl.ds(2 * j + c, DEVS, stride=8), :] = part[
                    row : row + DEVS, h * 128 : h * 128 + 128
                ]

    @pl.when(j == 3)
    def _():
        for h in range(4):
            out_ref[:, h * 128 : h * 128 + 128] = sum_ref[h].astype(bf16)


def interpolate_kernel(meta_ref, recv_ref, table_ref, packed_ref, out_ref, flag_ref, grid_ref, result_ref):
    grid = jnp.dot(table_ref[...], recv_ref[...], preferred_element_type=f32)
    flag_ref[...] = jnp.where(jnp.isnan(grid[:8, :128]), 1.0, 0.0)
    grid = grid.T
    high = grid.astype(bf16)
    grid_ref[0] = high
    grid_ref[1] = (grid - high.astype(f32)).astype(bf16)
    result_ref[...] = jnp.zeros_like(result_ref)

    def tile(r, _):
        at = pl.ds(pl.multiple_of(r * TILE, TILE), TILE)
        fields = packed_ref[:, at]
        y = fields[19:20].astype(jnp.int32)
        z = fields[20:21].astype(jnp.int32)
        away = iota((M, TILE), 0) - y
        is0, is1, is2 = away == 0, away == 1, away == 2
        total = jnp.zeros((M, TILE), f32)
        for c in range(3):
            hot = hot_z(z, c)
            near = jnp.dot(grid_ref[0], hot, preferred_element_type=f32) + jnp.dot(
                grid_ref[1], hot, preferred_element_type=f32
            )
            for xp in range(2):
                w = [fields[xp * 9 + b * 3 + c : xp * 9 + b * 3 + c + 1] for b in range(3)]
                v = jnp.where(is0, w[0], jnp.where(is1, w[1], jnp.where(is2, w[2], 0.0)))
                total = total + v * near[xp * M : (xp + 1) * M]
        result_ref[:, at] = jnp.broadcast_to(jnp.sum(total, axis=0, keepdims=True), (8, TILE))
        return 0

    lax.fori_loop(0, (meta_ref[PENS] + TILE - 1) // TILE, tile, 0)
    width = SLOTS + 128
    for s in range(PENS):
        start = meta_ref[s]
        piece = result_ref[:, pl.ds(pl.multiple_of(start // 128 * 128, 128), width)]
        piece = pltpu.roll(piece, (width - start % 128) % width, 1)
        out_ref[s : s + 1, :] = piece[0:1, :SLOTS]


def collect_kernel(back_ref, route_ref, out_ref):
    back = back_ref[...]
    high = back.astype(bf16)
    low = (back - high.astype(f32)).astype(bf16)
    both = jnp.concatenate([high.astype(f32), low.astype(f32)], axis=0).astype(bf16)
    step = 512
    for k in range(4):
        at = slice(k * step, k * step + step)
        owner = route_ref[0:1, at]
        slot = iota((SLOTS, step), 0)
        pen = iota((PENS, step), 0)
        total = jnp.zeros((PENS, step), f32)
        for shift in range(2):
            hot = jnp.where(slot == route_ref[shift + 1 : shift + 2, at], 1.0, 0.0).astype(bf16)
            got = jnp.dot(both, hot, preferred_element_type=f32)
            total = total + jnp.where(pen == owner + shift, got[:PENS] + got[PENS:], 0.0)
        out_ref[:, at] = jnp.broadcast_to(jnp.sum(total, axis=0, keepdims=True), (8, step))


def struct(shape, dtype):
    return jax.ShapeDtypeStruct(shape, dtype)


def whole(count):
    return [pl.BlockSpec(memory_space=pltpu.VMEM)] * count


SMEM = pl.BlockSpec(memory_space=pltpu.SMEM)
LIMIT = pltpu.CompilerParams(vmem_limit_bytes=40 * 1024 * 1024)


def far_field_blocks(charges, stencil, corner_cells, cluster_sizes, green_spectrum):
    along_z, along_y, along_x, back_y, back_x, back_z = [jnp.asarray(t) for t in tables()]
    slab = lax.axis_index("clus").astype(jnp.int32).reshape(1)
    green = green_spectrum.transpose(1, 2, 0).reshape(-1, L)
    sent, route = pl.pallas_call(
        bucket_kernel,
        out_shape=[
            struct((PENS, ROWS, SLOTS), bf16),
            struct((8, 8 * CAP), jnp.int32),
        ],
        in_specs=[SMEM, SMEM] + whole(3),
        out_specs=whole(2),
        scratch_shapes=[
            pltpu.VMEM((ROWS, 8 * CAP), f32),
            pltpu.VMEM((ROWS, 8 * CAP), f32),
            pltpu.VMEM((ROWS * PENS, SLOTS), f32),
        ],
        compiler_params=LIMIT,
        name="bucket",
    )(
        slab,
        cluster_sizes,
        charges.reshape(8, CAP),
        stencil,
        corner_cells,
    )
    green, sent = lax.optimization_barrier((green, sent))
    pieces = pl.pallas_call(
        recut_kernel,
        grid=(4,),
        out_shape=[struct((4, L // 8, L), bf16)] * 8,
        in_specs=[SMEM, pl.BlockSpec((L // 8 * 32, 128), lambda j: (0, j))],
        out_specs=[pl.BlockSpec((4, L // 8, 128), lambda j: (0, 0, j))] * 8,
        compiler_params=LIMIT,
        name="recut",
    )(slab, green)
    recv = lax.all_to_all(sent, "pen", 0, 0, tiled=True)
    pieces = [pieces[0]] + [
        lax.ppermute(pieces[s], "clus", [(a, (a + s) % 8) for a in range(8)])
        for s in range(1, 8)
    ]
    section, packed, meta = pl.pallas_call(
        deposit_kernel,
        out_shape=[
            struct((2 * L, 2 * M), bf16),
            struct((FIELDS, ROOM), f32),
            struct((PENS + 1,), jnp.int32),
        ],
        in_specs=whole(2),
        out_specs=whole(2) + [SMEM],
        scratch_shapes=[
            pltpu.VMEM((M, 3 * TILE), bf16),
            pltpu.VMEM((2 * M, 3 * TILE), bf16),
            pltpu.VMEM((2 * M, 3 * TILE), bf16),
            pltpu.VMEM((M, 2 * M), f32),
        ],
        compiler_params=LIMIT,
        name="deposit",
    )(recv, along_z)
    section, *pieces = lax.optimization_barrier((section, *pieces))
    section = lax.all_to_all(
        section.reshape(DEVS, 8, 2 * M), ("clus", "pen"), 0, 0, tiled=True
    )
    section = pl.pallas_call(
        convolve_kernel,
        grid=(4,),
        out_shape=struct((2 * L, 2 * M), bf16),
        in_specs=[
            SMEM,
            pl.BlockSpec((2 * L, 2 * M), lambda j: (0, 0)),
        ]
        + [pl.BlockSpec((1, L // 8, L), lambda j: (j, 0, 0))] * 8
        + [
            pl.BlockSpec((2 * L, 2 * M), lambda j: (0, 0)),
            pl.BlockSpec((2 * M, 2 * L), lambda j: (0, 0)),
            pl.BlockSpec((2 * M, 2 * L), lambda j: (0, 0)),
            pl.BlockSpec((2 * M, 2 * L), lambda j: (0, 0)),
        ],
        out_specs=pl.BlockSpec((2 * L, 2 * M), lambda j: (0, 0)),
        scratch_shapes=[
            pltpu.VMEM((4, 2 * L, 128), f32),
            pltpu.VMEM((4, 2 * L, 128), f32),
            pltpu.VMEM((8, L // 8, L), bf16),
        ],
        compiler_params=LIMIT,
        name="convolve",
    )(slab, section.reshape(2 * L, 2 * M), *pieces, along_y, along_x, back_y, back_x)
    section = lax.all_to_all(
        section.reshape(DEVS, 8, 2 * M), ("clus", "pen"), 0, 0, tiled=True
    )
    back, flag = pl.pallas_call(
        interpolate_kernel,
        out_shape=[struct((PENS, SLOTS), f32), struct((8, 128), f32)],
        in_specs=[SMEM] + whole(3),
        out_specs=whole(2),
        scratch_shapes=[pltpu.VMEM((2, 2 * M, M), bf16), pltpu.VMEM((8, ROOM), f32)],
        compiler_params=LIMIT,
        name="interpolate",
    )(meta, section.reshape(2 * L, 2 * M), back_z, packed)
    back = lax.all_to_all(back, "pen", 0, 0, tiled=True)
    far = pl.pallas_call(
        collect_kernel,
        out_shape=struct((8, 8 * CAP), f32),
        in_specs=whole(2),
        out_specs=pl.BlockSpec(memory_space=pltpu.VMEM),
        compiler_params=LIMIT,
        name="collect",
    )(back, route)
    pool = jnp.concatenate(
        [recv[:, 42:48, :CAP], recv[:, 42:46, CAP:].reshape(PENS, 2, CAP)], axis=1
    ).reshape(PENS * 8, CAP)
    return far[0], pool, flag[0, 0]


def neighbours(x, axis):
    devices = lax.axis_size(axis)
    up = [(i, i + 1) for i in range(devices - 1)]
    before = lax.ppermute(x, axis, up)
    after = lax.ppermute(x, axis, [(j, i) for i, j in up])
    return jnp.concatenate([before, x, after], axis=0)


def per_device(
    charges, stencil, corner_cells, cluster_sizes, near_source, near_blocks, green_spectrum
):
    slot_rank = jnp.arange(CAP, dtype=jnp.int32)
    slot_mask = (slot_rank[None, :] < cluster_sizes[:, None]).reshape(-1)
    far_field, pool, overflow = far_field_blocks(
        charges, stencil, corner_cells, cluster_sizes, green_spectrum
    )
    local_source = near_source - (lax.axis_index("clus") - 1) * pool.shape[0]
    source_rows = neighbours(pool, "clus")[local_source]
    near_terms = jnp.einsum(
        "pjm,pm->pj", near_blocks, source_rows, preferred_element_type=f32
    )
    near_field = near_terms.reshape(-1, NB, CAP).sum(axis=1).reshape(-1)

    def general():
        charge_value = jnp.where(slot_mask, charges, jnp.zeros_like(charges)).astype(f32)
        return far_field_general(charge_value, stencil, corner_cells, green_spectrum)

    far_field = lax.cond(overflow > 0.0, general, lambda: far_field)
    total = far_field + near_field
    return jnp.where(slot_mask, total, jnp.zeros_like(total))


def solution(mesh):
    in_specs = (
        P(("clus", "pen")),
        P(None, ("clus", "pen")),
        P(None, ("clus", "pen")),
        P(("clus", "pen")),
        P(("clus", "pen")),
        P(("clus", "pen"), None, None),
        P(None, "clus", "pen"),
    )
    out_specs = P(("clus", "pen"))
    return jax.shard_map(
        per_device, mesh=mesh, in_specs=in_specs, out_specs=out_specs, check_vma=False
    )
```

```python
import functools
import math

import jax
import jax.numpy as jnp
import ml_dtypes
import numpy as np
from jax import lax
from jax.experimental import pallas as pl
from jax.experimental.pallas import tpu as pltpu
from jax.sharding import PartitionSpec as P

M = 256
L = 512
CAP = 256
NB = 4
SLOTS = 384
PENS = 16
DEVS = 128
ROOM = PENS * SLOTS + 512
TILE = 512
ROWS = 48
FIELDS = 24

exact = lax.Precision.HIGHEST
f32 = jnp.float32
bf16 = jnp.bfloat16
NT = (((1,), (1,)), ((), ()))


def section_table(count, length, sign):
    sample = jnp.arange(count, dtype=jnp.int32)[:, None]
    wave_number = jnp.arange(length, dtype=jnp.int32)[None, :]
    phase = (sample * wave_number % length).astype(jnp.float32) * (2.0 * math.pi / length)
    cosine = jnp.cos(phase)
    sine = jnp.sin(phase)
    from_real = jnp.stack([cosine, sign * sine], axis=1)
    from_imag = jnp.stack([-sign * sine, cosine], axis=1)
    return jnp.stack([from_real, from_imag], axis=0)


def exchanged(x, axis, split):
    return lax.all_to_all(x.astype(bf16), axis, split_axis=split, concat_axis=split + 1, tiled=True)


def far_field_general(charge_value, stencil, corner_cells, green_spectrum):
    pen_count = lax.axis_size("pen")
    clus_count = lax.axis_size("clus")
    planes = M // clus_count
    rows_own = M // pen_count
    pen_spread = L // pen_count
    clus_spread = L // clus_count
    slab_index = lax.axis_index("clus")
    forward_table = section_table(M, L, -1.0)
    inverse_table = section_table(M, L, 1.0)
    offset = jnp.arange(27, dtype=jnp.int32)[:, None]
    first = corner_cells[0][None, :] + offset // 9 - slab_index * planes
    second = corner_cells[1][None, :] + offset // 3 % 3
    third = corner_cells[2][None, :] + offset % 3
    slab_cell = (first * M + second) * M + third
    deposit = stencil * charge_value[None, :]
    slab_charge = (
        jnp.zeros((planes * M * M,), f32).at[slab_cell.reshape(-1)].add(deposit.reshape(-1))
    )
    grid_block = slab_charge.reshape(planes, pen_count, rows_own, M).transpose(1, 0, 2, 3)
    grid_block = lax.all_to_all(grid_block, "pen", 0, 0, tiled=True).sum(axis=0)
    section = jnp.einsum("xyz,zdk->dxyk", grid_block, forward_table[0], precision=exact)
    section = (
        section.reshape(2, planes, rows_own, pen_count, pen_spread)
        .transpose(0, 3, 2, 1, 4)
        .reshape(2, pen_count, rows_own, planes * pen_spread)
    )
    section = exchanged(section, "pen", 1).reshape(2, M, planes * pen_spread).astype(f32)
    section = jnp.einsum("cyw,cydk->dkw", section, forward_table, precision=exact)
    section = (
        section.reshape(2, clus_count, clus_spread, planes, pen_spread)
        .transpose(0, 1, 3, 2, 4)
        .reshape(2, clus_count, planes, clus_spread * pen_spread)
    )
    section = exchanged(section, "clus", 1).reshape(2, M, clus_spread * pen_spread).astype(f32)
    spectrum = jnp.einsum("cxv,cxdk->dkv", section, forward_table, precision=exact)
    spectrum = spectrum * green_spectrum.reshape(1, L, clus_spread * pen_spread)
    section = jnp.einsum("ckv,cxdk->dxv", spectrum, inverse_table, precision=exact)
    section = (
        section.reshape(2, clus_count, planes, clus_spread, pen_spread)
        .transpose(0, 1, 3, 2, 4)
        .reshape(2, clus_count, clus_spread, planes * pen_spread)
    )
    section = exchanged(section, "clus", 1).reshape(2, L, planes * pen_spread).astype(f32)
    section = jnp.einsum("ckw,cydk->dyw", section, inverse_table, precision=exact)
    section = (
        section.reshape(2, pen_count, rows_own, planes, pen_spread)
        .transpose(0, 1, 4, 2, 3)
        .reshape(2, pen_count, pen_spread, rows_own * planes)
    )
    section = exchanged(section, "pen", 1).reshape(2, L, rows_own * planes).astype(f32)
    lines = jnp.einsum("ckw,czk->zw", section, inverse_table[:, :, 0, :], precision=exact)
    lines = lines * (1.0 / (L * L * L))
    block = lines.reshape(M, rows_own, planes).transpose(2, 1, 0)
    slab = jnp.broadcast_to(block[None], (pen_count,) + block.shape)
    slab = lax.all_to_all(slab, "pen", 0, 0, tiled=True).transpose(1, 0, 2, 3)
    return jnp.sum(stencil * slab.reshape(-1)[slab_cell], axis=0)


def rounded(x):
    return x.astype(np.float32).astype(ml_dtypes.bfloat16).astype(np.float64)


def balanced(exact_values):
    near = rounded(exact_values)
    ulp = np.ldexp(1.0, np.frexp(exact_values)[1] - 8)
    error = near - exact_values
    other = near - np.sign(error) * ulp
    gain = (other - near) * exact_values
    cost = (other - exact_values) ** 2 - error**2
    for x in range(exact_values.shape[1]):
        bias = np.sum(error[:, x] * exact_values[:, x])
        order = np.argsort(cost[:, x] / np.maximum(np.abs(gain[:, x]), 1e-30))
        for i in order:
            if error[i, x] != 0.0 and np.abs(bias + gain[i, x]) < np.abs(bias):
                near[i, x] = other[i, x]
                bias += gain[i, x]
            if np.abs(bias) < 1e-4:
                break
    return near


@functools.cache
def tables():
    plane = np.concatenate([2 * np.arange(DEVS), 2 * np.arange(DEVS) + 1])
    own = np.arange(L).reshape(PENS, 8, 4).transpose(1, 0, 2).reshape(-1)
    phase = (np.outer(np.arange(L), np.arange(M)) % L) * (2.0 * np.pi / L)
    both = balanced(np.concatenate([np.cos(phase), np.sin(phase)], axis=0))
    cos, sin = both[:L], both[L:]
    along_z = np.stack([cos[own], -sin[own]], axis=1).reshape(2 * L, M)
    back_z = along_z.T / float(L) ** 3
    along_y = np.block([[cos, sin], [-sin, cos]])
    back_y = along_y.T
    cos, sin = cos.T[plane], sin.T[plane]
    along_x = np.block([[cos, -sin], [sin, cos]])
    back_x = along_x
    return tuple(
        t.astype(np.float32).astype(ml_dtypes.bfloat16)
        for t in (along_z, along_y, along_x, back_y, back_x, back_z)
    )


def iota(shape, dim):
    return lax.broadcasted_iota(jnp.int32, shape, dim)


def bucket_kernel(
    slab_ref, sizes_ref, charge_ref, stencil_ref, corner_ref, out_ref, route_ref,
    first_ref, second_ref, total_ref,
):
    count = 8 * CAP
    lane = iota((1, CAP), 1)
    charge = charge_ref[...].astype(f32)
    live = jnp.concatenate(
        [jnp.where(lane < sizes_ref[k], 1.0, 0.0) for k in range(8)], axis=1
    )
    row8 = iota((8, CAP), 0)
    size8 = jnp.zeros((8, CAP), jnp.int32)
    for k in range(8):
        size8 = jnp.where(row8 == k, sizes_ref[k], size8)
    charge = jnp.where(iota((8, CAP), 1) < size8, charge, 0.0)
    q = jnp.concatenate([charge[k : k + 1] for k in range(8)], axis=1)
    x = corner_ref[0:1, :] - slab_ref[0] * 32
    owner = jnp.where(live > 0.0, x >> 1, -2)
    odd = (x & 1) == 1
    pen = iota((PENS, count), 0)
    member = jnp.where((pen == owner) | (pen == owner + 1), 1.0, 0.0)
    upper = jnp.where(iota((128, 128), 0) <= iota((128, 128), 1), 1.0, 0.0).astype(bf16)
    carry = jnp.zeros((PENS, 128), f32)
    ranks = []
    for k in range(count // 128):
        part = member[:, 128 * k : 128 * k + 128]
        upto = jnp.dot(part.astype(bf16), upper, preferred_element_type=f32) + carry
        ranks.append(upto - part)
        carry = jnp.broadcast_to(upto[:, 127:128], (PENS, 128))
    rank = jnp.concatenate(ranks, axis=1)
    over = jnp.where(jnp.max(carry, axis=0, keepdims=True) > SLOTS, 1.0, 0.0)
    over = jnp.concatenate([over] * (SLOTS // 128), axis=1)
    pos_first = jnp.sum(jnp.where(pen == owner, rank, 0.0), axis=0, keepdims=True)
    pos_second = jnp.sum(jnp.where(pen == owner + 1, rank, 0.0), axis=0, keepdims=True)
    pos_first = jnp.where(live > 0.0, pos_first, -1.0).astype(jnp.int32)
    pos_second = jnp.where(live > 0.0, pos_second, -1.0).astype(jnp.int32)
    route_ref[...] = jnp.zeros((8, count), jnp.int32)
    route_ref[0:1, :] = owner
    route_ref[1:2, :] = pos_first
    route_ref[2:3, :] = pos_second

    for ref in (first_ref, second_ref):
        ref[...] = jnp.zeros((ROWS, count), f32)
        ref[18:19, :] = q
        ref[19:20, :] = corner_ref[1:2, :].astype(f32)
        ref[20:21, :] = corner_ref[2:3, :].astype(f32)
        ref[21:22, :] = live
    w0 = stencil_ref[0:9, :]
    w1 = stencil_ref[9:18, :]
    w2 = stencil_ref[18:27, :]
    first_ref[0:9, :] = jnp.where(odd, 0.0, w0)
    first_ref[9:18, :] = jnp.where(odd, w0, w1)
    second_ref[0:9, :] = jnp.where(odd, w1, w2)
    second_ref[9:18, :] = jnp.where(odd, w2, 0.0)
    for ref in (first_ref, second_ref):
        w = ref[0:18, :]
        ref[24:42, :] = w - w.astype(bf16).astype(f32)

    step = 512
    total_ref[...] = jnp.zeros_like(total_ref)

    def chunk(k, _):
        at = pl.ds(pl.multiple_of(k * step, step), step)
        own = route_ref[0:1, at]
        slot = iota((SLOTS, step), 0)
        for ref, shift, row in ((first_ref, 0, 1), (second_ref, 1, 2)):
            values = ref[:, at].astype(bf16)
            spread = jnp.concatenate(
                [
                    values * jnp.where(own + shift == p, 1.0, 0.0).astype(bf16)
                    for p in range(PENS)
                ],
                axis=0,
            )
            hot = jnp.where(slot == route_ref[row : row + 1, at], 1.0, 0.0).astype(bf16)
            total_ref[...] += lax.dot_general(spread, hot, NT, preferred_element_type=f32)
        return 0

    lax.fori_loop(0, count // step, chunk, 0)
    first_ref[...] = jnp.zeros_like(first_ref)
    first_ref[22:23, 0:SLOTS] = over
    first_ref[42:48, 0:CAP] = charge[0:6]
    for k in range(4):
        half = slice(k % 2 * 128, k % 2 * 128 + 128)
        first_ref[42 + k : 43 + k, CAP:SLOTS] = charge[6 + k // 2 : 7 + k // 2, half]
    extra = first_ref[:, 0:SLOTS]
    for p in range(PENS):
        out_ref[p] = (total_ref[ROWS * p : ROWS * p + ROWS, :] + extra).astype(bf16)


def rows_as_bf16():
    return iota((M, TILE), 0).astype(f32).astype(bf16)


def hot_z(z, c):
    one = jnp.ones((M, TILE), bf16)
    return jnp.where(rows_as_bf16() == (z + c).astype(f32).astype(bf16), one, jnp.zeros_like(one))


def deposit_kernel(
    recv_ref, table_ref, out_ref, packed_ref, meta_ref, left_ref, right_ref,
    low_ref, grid_ref,
):
    packed_ref[...] = jnp.zeros_like(packed_ref)
    blocks = [recv_ref[s].astype(f32) for s in range(PENS)]
    counts = [jnp.sum(b[21:22, :]).astype(jnp.int32) for b in blocks]
    start = jnp.int32(0)
    for s in range(PENS):
        meta_ref[s] = start
        block = blocks[s][:FIELDS] + jnp.concatenate(
            [blocks[s][FIELDS : FIELDS + 18], jnp.zeros((FIELDS - 18, SLOTS), f32)], axis=0
        )
        block = jnp.concatenate([block, jnp.zeros((FIELDS, 128), f32)], axis=1)
        block = pltpu.roll(block, start % 128, 1)
        at = pl.ds(pl.multiple_of(start // 128 * 128, 128), SLOTS + 128)
        packed_ref[:, at] = packed_ref[:, at] + block
        start = start + counts[s]
    meta_ref[PENS] = start
    over = blocks[0][22:23, :128]
    for s in range(1, PENS):
        over = jnp.maximum(over, blocks[s][22:23, :128])
    spoil = jnp.where(over[:, :1] > 0.0, jnp.nan, 0.0)
    grid_ref[...] = jnp.zeros_like(grid_ref)

    def tile(r, _):
        fields = packed_ref[:, pl.ds(pl.multiple_of(r * TILE, TILE), TILE)]
        y = fields[19:20].astype(jnp.int32)
        z = fields[20:21].astype(jnp.int32)
        weights = fields[0:18] * fields[18:19]
        high = weights.astype(bf16)
        low = (weights - high.astype(f32)).astype(bf16)
        place = rows_as_bf16()
        at0, at1, at2 = [place == (y + b).astype(f32).astype(bf16) for b in range(3)]
        zero = jnp.zeros((M, TILE), bf16)
        for c in range(3):
            left_ref[:, c * TILE : (c + 1) * TILE] = hot_z(z, c)
            for xp in range(2):
                for part, ref in ((high, right_ref), (low, low_ref)):
                    w = [part[xp * 9 + b * 3 + c : xp * 9 + b * 3 + c + 1] for b in range(3)]
                    v = jnp.where(at0, w[0], jnp.where(at1, w[1], jnp.where(at2, w[2], zero)))
                    ref[xp * M : (xp + 1) * M, c * TILE : (c + 1) * TILE] = v
        left = left_ref[...]
        grid_ref[...] += lax.dot_general(
            left, right_ref[...], NT, preferred_element_type=f32
        ) + lax.dot_general(left, low_ref[...], NT, preferred_element_type=f32)
        return 0

    lax.fori_loop(0, (start + TILE - 1) // TILE, tile, 0)
    grid = grid_ref[...] + spoil
    high = grid.astype(bf16)
    low = (grid - high.astype(f32)).astype(bf16)
    for k in range(4):
        at = slice(k * 256, k * 256 + 256)
        table = table_ref[at, :]
        out_ref[at, :] = (
            jnp.dot(table, high, preferred_element_type=f32)
            + jnp.dot(table, low, preferred_element_type=f32)
        ).astype(bf16)


def recut_kernel(slab_ref, green_ref, *out_refs):
    for s, ref in enumerate(out_refs):
        first = (slab_ref[0] + s) % 8 * 4
        for c in range(4):
            ref[c] = green_ref[pl.ds(first + c, L // 8, stride=32), :].astype(bf16)


def convolve_kernel(
    slab_ref, recv_ref, g0_ref, g1_ref, g2_ref, g3_ref, g4_ref, g5_ref, g6_ref, g7_ref, along_y_ref, along_x_ref, back_y_ref, back_x_ref, out_ref, in_ref, sum_ref, green_ref
):
    j = pl.program_id(0)

    @pl.when(j == 0)
    def _():
        for h in range(4):
            in_ref[h] = recv_ref[:, h * 128 : h * 128 + 128].astype(f32)

    for s, ref in enumerate((g0_ref, g1_ref, g2_ref, g3_ref, g4_ref, g5_ref, g6_ref, g7_ref)):
        for i in range(2):
            green_ref[i, (slab_ref[0] + 8 - s) % 8] = ref[i]

    def piece(i, xp):
        return jnp.concatenate(
            [
                in_ref[2 * xp + h, pl.ds(4 * j + 2 * i + c, DEVS, stride=8), :].astype(bf16)
                for c in range(2)
                for h in range(2)
            ],
            axis=1,
        )

    both = [jnp.concatenate([piece(i, 0), piece(i, 1)], axis=0) for i in range(2)]
    both = [
        lax.dot_general(along_y_ref[...], t, NT, preferred_element_type=f32).astype(bf16)
        for t in both
    ]
    both = [
        jnp.dot(
            jnp.concatenate([t[:L], t[L:]], axis=1),
            along_x_ref[...],
            preferred_element_type=f32,
        )
        for t in both
    ]
    greens = [green_ref[i].reshape(L, L).astype(f32) for i in range(2)]
    both = [
        jnp.concatenate([(t[:, :L] * g).astype(bf16), (t[:, L:] * g).astype(bf16)], axis=0)
        for t, g in zip(both, greens)
    ]
    both = [
        jnp.dot(back_y_ref[...], t, preferred_element_type=f32).astype(bf16) for t in both
    ]
    both = [
        lax.dot_general(
            back_x_ref[...],
            jnp.concatenate([t[:M], t[M:]], axis=1),
            NT,
            preferred_element_type=f32,
        )
        for t in both
    ]
    for i in range(2):
        for c in range(2):
            for xp in range(2):
                row = c * M + xp * DEVS
                for h in range(2):
                    sum_ref[2 * xp + h, pl.ds(4 * j + 2 * i + c, DEVS, stride=8), :] = both[i][
                        row : row + DEVS, h * 128 : h * 128 + 128
                    ]

    @pl.when(j == 1)
    def _():
        for h in range(4):
            out_ref[:, h * 128 : h * 128 + 128] = sum_ref[h].astype(bf16)


def interpolate_kernel(meta_ref, recv_ref, table_ref, packed_ref, out_ref, flag_ref, grid_ref, result_ref):
    grid = jnp.dot(table_ref[...], recv_ref[...], preferred_element_type=f32)
    flag_ref[...] = jnp.where(jnp.isnan(grid[:8, :128]), 1.0, 0.0)
    grid = grid.T
    high = grid.astype(bf16)
    grid_ref[0] = high
    grid_ref[1] = (grid - high.astype(f32)).astype(bf16)
    result_ref[...] = jnp.zeros_like(result_ref)

    def tile(r, _):
        at = pl.ds(pl.multiple_of(r * TILE, TILE), TILE)
        fields = packed_ref[:, at]
        y = fields[19:20].astype(jnp.int32)
        z = fields[20:21].astype(jnp.int32)
        away = iota((M, TILE), 0) - y
        is0, is1, is2 = away == 0, away == 1, away == 2
        total = jnp.zeros((M, TILE), f32)
        for c in range(3):
            hot = hot_z(z, c)
            near = jnp.dot(grid_ref[0], hot, preferred_element_type=f32) + jnp.dot(
                grid_ref[1], hot, preferred_element_type=f32
            )
            for xp in range(2):
                w = [fields[xp * 9 + b * 3 + c : xp * 9 + b * 3 + c + 1] for b in range(3)]
                v = jnp.where(is0, w[0], jnp.where(is1, w[1], jnp.where(is2, w[2], 0.0)))
                total = total + v * near[xp * M : (xp + 1) * M]
        result_ref[:, at] = jnp.broadcast_to(jnp.sum(total, axis=0, keepdims=True), (8, TILE))
        return 0

    lax.fori_loop(0, (meta_ref[PENS] + TILE - 1) // TILE, tile, 0)
    width = SLOTS + 128
    for s in range(PENS):
        start = meta_ref[s]
        piece = result_ref[:, pl.ds(pl.multiple_of(start // 128 * 128, 128), width)]
        piece = pltpu.roll(piece, (width - start % 128) % width, 1)
        out_ref[s : s + 1, :] = piece[0:1, :SLOTS]


def collect_kernel(back_ref, route_ref, out_ref):
    back = back_ref[...]
    high = back.astype(bf16)
    low = (back - high.astype(f32)).astype(bf16)
    both = jnp.concatenate([high.astype(f32), low.astype(f32)], axis=0).astype(bf16)
    step = 512
    for k in range(4):
        at = slice(k * step, k * step + step)
        owner = route_ref[0:1, at]
        slot = iota((SLOTS, step), 0)
        pen = iota((PENS, step), 0)
        total = jnp.zeros((PENS, step), f32)
        for shift in range(2):
            hot = jnp.where(slot == route_ref[shift + 1 : shift + 2, at], 1.0, 0.0).astype(bf16)
            got = jnp.dot(both, hot, preferred_element_type=f32)
            total = total + jnp.where(pen == owner + shift, got[:PENS] + got[PENS:], 0.0)
        out_ref[:, at] = jnp.broadcast_to(jnp.sum(total, axis=0, keepdims=True), (8, step))


def struct(shape, dtype):
    return jax.ShapeDtypeStruct(shape, dtype)


def whole(count):
    return [pl.BlockSpec(memory_space=pltpu.VMEM)] * count


SMEM = pl.BlockSpec(memory_space=pltpu.SMEM)
LIMIT = pltpu.CompilerParams(vmem_limit_bytes=40 * 1024 * 1024)


def far_field_blocks(charges, stencil, corner_cells, cluster_sizes, green_spectrum):
    along_z, along_y, along_x, back_y, back_x, back_z = [jnp.asarray(t) for t in tables()]
    slab = lax.axis_index("clus").astype(jnp.int32).reshape(1)
    green = green_spectrum.transpose(1, 2, 0).reshape(-1, L)
    sent, route = pl.pallas_call(
        bucket_kernel,
        out_shape=[
            struct((PENS, ROWS, SLOTS), bf16),
            struct((8, 8 * CAP), jnp.int32),
        ],
        in_specs=[SMEM, SMEM] + whole(3),
        out_specs=whole(2),
        scratch_shapes=[
            pltpu.VMEM((ROWS, 8 * CAP), f32),
            pltpu.VMEM((ROWS, 8 * CAP), f32),
            pltpu.VMEM((ROWS * PENS, SLOTS), f32),
        ],
        compiler_params=LIMIT,
        name="bucket",
    )(
        slab,
        cluster_sizes,
        charges.reshape(8, CAP),
        stencil,
        corner_cells,
    )
    green, sent = lax.optimization_barrier((green, sent))
    pieces = pl.pallas_call(
        recut_kernel,
        grid=(4,),
        out_shape=[struct((4, L // 8, L), bf16)] * 8,
        in_specs=[SMEM, pl.BlockSpec((L // 8 * 32, 128), lambda j: (0, j))],
        out_specs=[pl.BlockSpec((4, L // 8, 128), lambda j: (0, 0, j))] * 8,
        compiler_params=LIMIT,
        name="recut",
    )(slab, green)
    recv = lax.all_to_all(sent, "pen", 0, 0, tiled=True)
    pieces = [pieces[0]] + [
        lax.ppermute(pieces[s], "clus", [(a, (a + s) % 8) for a in range(8)])
        for s in range(1, 8)
    ]
    section, packed, meta = pl.pallas_call(
        deposit_kernel,
        out_shape=[
            struct((2 * L, 2 * M), bf16),
            struct((FIELDS, ROOM), f32),
            struct((PENS + 1,), jnp.int32),
        ],
        in_specs=whole(2),
        out_specs=whole(2) + [SMEM],
        scratch_shapes=[
            pltpu.VMEM((M, 3 * TILE), bf16),
            pltpu.VMEM((2 * M, 3 * TILE), bf16),
            pltpu.VMEM((2 * M, 3 * TILE), bf16),
            pltpu.VMEM((M, 2 * M), f32),
        ],
        compiler_params=LIMIT,
        name="deposit",
    )(recv, along_z)
    section, *pieces = lax.optimization_barrier((section, *pieces))
    section = lax.all_to_all(
        section.reshape(DEVS, 8, 2 * M), ("clus", "pen"), 0, 0, tiled=True
    )
    section = pl.pallas_call(
        convolve_kernel,
        grid=(2,),
        out_shape=struct((2 * L, 2 * M), bf16),
        in_specs=[
            SMEM,
            pl.BlockSpec((2 * L, 2 * M), lambda j: (0, 0)),
        ]
        + [pl.BlockSpec((2, L // 8, L), lambda j: (j, 0, 0))] * 8
        + [
            pl.BlockSpec((2 * L, 2 * M), lambda j: (0, 0)),
            pl.BlockSpec((2 * M, 2 * L), lambda j: (0, 0)),
            pl.BlockSpec((2 * M, 2 * L), lambda j: (0, 0)),
            pl.BlockSpec((2 * M, 2 * L), lambda j: (0, 0)),
        ],
        out_specs=pl.BlockSpec((2 * L, 2 * M), lambda j: (0, 0)),
        scratch_shapes=[
            pltpu.VMEM((4, 2 * L, 128), f32),
            pltpu.VMEM((4, 2 * L, 128), f32),
            pltpu.VMEM((2, 8, L // 8, L), bf16),
        ],
        compiler_params=LIMIT,
        name="convolve",
    )(slab, section.reshape(2 * L, 2 * M), *pieces, along_y, along_x, back_y, back_x)
    section = lax.all_to_all(
        section.reshape(DEVS, 8, 2 * M), ("clus", "pen"), 0, 0, tiled=True
    )
    back, flag = pl.pallas_call(
        interpolate_kernel,
        out_shape=[struct((PENS, SLOTS), f32), struct((8, 128), f32)],
        in_specs=[SMEM] + whole(3),
        out_specs=whole(2),
        scratch_shapes=[pltpu.VMEM((2, 2 * M, M), bf16), pltpu.VMEM((8, ROOM), f32)],
        compiler_params=LIMIT,
        name="interpolate",
    )(meta, section.reshape(2 * L, 2 * M), back_z, packed)
    back = lax.all_to_all(back, "pen", 0, 0, tiled=True)
    far = pl.pallas_call(
        collect_kernel,
        out_shape=struct((8, 8 * CAP), f32),
        in_specs=whole(2),
        out_specs=pl.BlockSpec(memory_space=pltpu.VMEM),
        compiler_params=LIMIT,
        name="collect",
    )(back, route)
    pool = jnp.concatenate(
        [recv[:, 42:48, :CAP], recv[:, 42:46, CAP:].reshape(PENS, 2, CAP)], axis=1
    ).reshape(PENS * 8, CAP)
    return far[0], pool, flag[0, 0]


def neighbours(x, axis):
    devices = lax.axis_size(axis)
    up = [(i, i + 1) for i in range(devices - 1)]
    before = lax.ppermute(x, axis, up)
    after = lax.ppermute(x, axis, [(j, i) for i, j in up])
    return jnp.concatenate([before, x, after], axis=0)


def per_device(
    charges, stencil, corner_cells, cluster_sizes, near_source, near_blocks, green_spectrum
):
    slot_rank = jnp.arange(CAP, dtype=jnp.int32)
    slot_mask = (slot_rank[None, :] < cluster_sizes[:, None]).reshape(-1)
    far_field, pool, overflow = far_field_blocks(
        charges, stencil, corner_cells, cluster_sizes, green_spectrum
    )
    local_source = near_source - (lax.axis_index("clus") - 1) * pool.shape[0]
    source_rows = neighbours(pool, "clus")[local_source]
    near_terms = jnp.einsum(
        "pjm,pm->pj", near_blocks, source_rows, preferred_element_type=f32
    )
    near_field = near_terms.reshape(-1, NB, CAP).sum(axis=1).reshape(-1)

    def general():
        charge_value = jnp.where(slot_mask, charges, jnp.zeros_like(charges)).astype(f32)
        return far_field_general(charge_value, stencil, corner_cells, green_spectrum)

    far_field = lax.cond(overflow > 0.0, general, lambda: far_field)
    total = far_field + near_field
    return jnp.where(slot_mask, total, jnp.zeros_like(total))


def solution(mesh):
    in_specs = (
        P(("clus", "pen")),
        P(None, ("clus", "pen")),
        P(None, ("clus", "pen")),
        P(("clus", "pen")),
        P(("clus", "pen")),
        P(("clus", "pen"), None, None),
        P(None, "clus", "pen"),
    )
    out_specs = P(("clus", "pen"))
    return jax.shard_map(
        per_device, mesh=mesh, in_specs=in_specs, out_specs=out_specs, check_vma=False
    )
```

```python
import functools
import math

import jax
import jax.numpy as jnp
import ml_dtypes
import numpy as np
from jax import lax
from jax.experimental import pallas as pl
from jax.experimental.pallas import tpu as pltpu
from jax.sharding import PartitionSpec as P

M = 256
L = 512
CAP = 256
NB = 4
SLOTS = 384
PENS = 16
DEVS = 128
ROOM = PENS * SLOTS + 512
TILE = 512
ROWS = 48
FIELDS = 24

exact = lax.Precision.HIGHEST
f32 = jnp.float32
bf16 = jnp.bfloat16
NT = (((1,), (1,)), ((), ()))


def section_table(count, length, sign):
    sample = jnp.arange(count, dtype=jnp.int32)[:, None]
    wave_number = jnp.arange(length, dtype=jnp.int32)[None, :]
    phase = (sample * wave_number % length).astype(jnp.float32) * (2.0 * math.pi / length)
    cosine = jnp.cos(phase)
    sine = jnp.sin(phase)
    from_real = jnp.stack([cosine, sign * sine], axis=1)
    from_imag = jnp.stack([-sign * sine, cosine], axis=1)
    return jnp.stack([from_real, from_imag], axis=0)


def exchanged(x, axis, split):
    return lax.all_to_all(x.astype(bf16), axis, split_axis=split, concat_axis=split + 1, tiled=True)


def far_field_general(charge_value, stencil, corner_cells, green_spectrum):
    pen_count = lax.axis_size("pen")
    clus_count = lax.axis_size("clus")
    planes = M // clus_count
    rows_own = M // pen_count
    pen_spread = L // pen_count
    clus_spread = L // clus_count
    slab_index = lax.axis_index("clus")
    forward_table = section_table(M, L, -1.0)
    inverse_table = section_table(M, L, 1.0)
    offset = jnp.arange(27, dtype=jnp.int32)[:, None]
    first = corner_cells[0][None, :] + offset // 9 - slab_index * planes
    second = corner_cells[1][None, :] + offset // 3 % 3
    third = corner_cells[2][None, :] + offset % 3
    slab_cell = (first * M + second) * M + third
    deposit = stencil * charge_value[None, :]
    slab_charge = (
        jnp.zeros((planes * M * M,), f32).at[slab_cell.reshape(-1)].add(deposit.reshape(-1))
    )
    grid_block = slab_charge.reshape(planes, pen_count, rows_own, M).transpose(1, 0, 2, 3)
    grid_block = lax.all_to_all(grid_block, "pen", 0, 0, tiled=True).sum(axis=0)
    section = jnp.einsum("xyz,zdk->dxyk", grid_block, forward_table[0], precision=exact)
    section = (
        section.reshape(2, planes, rows_own, pen_count, pen_spread)
        .transpose(0, 3, 2, 1, 4)
        .reshape(2, pen_count, rows_own, planes * pen_spread)
    )
    section = exchanged(section, "pen", 1).reshape(2, M, planes * pen_spread).astype(f32)
    section = jnp.einsum("cyw,cydk->dkw", section, forward_table, precision=exact)
    section = (
        section.reshape(2, clus_count, clus_spread, planes, pen_spread)
        .transpose(0, 1, 3, 2, 4)
        .reshape(2, clus_count, planes, clus_spread * pen_spread)
    )
    section = exchanged(section, "clus", 1).reshape(2, M, clus_spread * pen_spread).astype(f32)
    spectrum = jnp.einsum("cxv,cxdk->dkv", section, forward_table, precision=exact)
    spectrum = spectrum * green_spectrum.reshape(1, L, clus_spread * pen_spread)
    section = jnp.einsum("ckv,cxdk->dxv", spectrum, inverse_table, precision=exact)
    section = (
        section.reshape(2, clus_count, planes, clus_spread, pen_spread)
        .transpose(0, 1, 3, 2, 4)
        .reshape(2, clus_count, clus_spread, planes * pen_spread)
    )
    section = exchanged(section, "clus", 1).reshape(2, L, planes * pen_spread).astype(f32)
    section = jnp.einsum("ckw,cydk->dyw", section, inverse_table, precision=exact)
    section = (
        section.reshape(2, pen_count, rows_own, planes, pen_spread)
        .transpose(0, 1, 4, 2, 3)
        .reshape(2, pen_count, pen_spread, rows_own * planes)
    )
    section = exchanged(section, "pen", 1).reshape(2, L, rows_own * planes).astype(f32)
    lines = jnp.einsum("ckw,czk->zw", section, inverse_table[:, :, 0, :], precision=exact)
    lines = lines * (1.0 / (L * L * L))
    block = lines.reshape(M, rows_own, planes).transpose(2, 1, 0)
    slab = jnp.broadcast_to(block[None], (pen_count,) + block.shape)
    slab = lax.all_to_all(slab, "pen", 0, 0, tiled=True).transpose(1, 0, 2, 3)
    return jnp.sum(stencil * slab.reshape(-1)[slab_cell], axis=0)


def rounded(x):
    return x.astype(np.float32).astype(ml_dtypes.bfloat16).astype(np.float64)


def balanced(exact_values):
    near = rounded(exact_values)
    ulp = np.ldexp(1.0, np.frexp(exact_values)[1] - 8)
    error = near - exact_values
    other = near - np.sign(error) * ulp
    gain = (other - near) * exact_values
    cost = (other - exact_values) ** 2 - error**2
    for x in range(exact_values.shape[1]):
        bias = np.sum(error[:, x] * exact_values[:, x])
        order = np.argsort(cost[:, x] / np.maximum(np.abs(gain[:, x]), 1e-30))
        for i in order:
            if error[i, x] != 0.0 and np.abs(bias + gain[i, x]) < np.abs(bias):
                near[i, x] = other[i, x]
                bias += gain[i, x]
            if np.abs(bias) < 1e-4:
                break
    return near


@functools.cache
def tables():
    plane = np.concatenate([2 * np.arange(DEVS), 2 * np.arange(DEVS) + 1])
    own = np.arange(L).reshape(PENS, 8, 4).transpose(1, 0, 2).reshape(-1)
    phase = (np.outer(np.arange(L), np.arange(M)) % L) * (2.0 * np.pi / L)
    both = balanced(np.concatenate([np.cos(phase), np.sin(phase)], axis=0))
    cos, sin = both[:L], both[L:]
    along_z = np.stack([cos[own], -sin[own]], axis=1).reshape(2 * L, M)
    back_z = along_z.T / float(L) ** 3
    along_y = np.block([[cos, sin], [-sin, cos]])
    back_y = along_y.T
    cos, sin = cos.T[plane], sin.T[plane]
    along_x = np.block([[cos, -sin], [sin, cos]])
    back_x = along_x
    return tuple(
        t.astype(np.float32).astype(ml_dtypes.bfloat16)
        for t in (along_z, along_y, along_x, back_y, back_x, back_z)
    )


def iota(shape, dim):
    return lax.broadcasted_iota(jnp.int32, shape, dim)


def bucket_kernel(
    slab_ref, sizes_ref, charge_ref, stencil_ref, corner_ref, out_ref, route_ref,
    first_ref, second_ref, total_ref,
):
    count = 8 * CAP
    lane = iota((1, CAP), 1)
    charge = charge_ref[...].astype(f32)
    live = jnp.concatenate(
        [jnp.where(lane < sizes_ref[k], 1.0, 0.0) for k in range(8)], axis=1
    )
    row8 = iota((8, CAP), 0)
    size8 = jnp.zeros((8, CAP), jnp.int32)
    for k in range(8):
        size8 = jnp.where(row8 == k, sizes_ref[k], size8)
    charge = jnp.where(iota((8, CAP), 1) < size8, charge, 0.0)
    q = jnp.concatenate([charge[k : k + 1] for k in range(8)], axis=1)
    x = corner_ref[0:1, :] - slab_ref[0] * 32
    owner = jnp.where(live > 0.0, x >> 1, -2)
    odd = (x & 1) == 1
    pen = iota((PENS, count), 0)
    member = jnp.where((pen == owner) | (pen == owner + 1), 1.0, 0.0)
    upper = jnp.where(iota((128, 128), 0) <= iota((128, 128), 1), 1.0, 0.0).astype(bf16)
    carry = jnp.zeros((PENS, 128), f32)
    ranks = []
    for k in range(count // 128):
        part = member[:, 128 * k : 128 * k + 128]
        upto = jnp.dot(part.astype(bf16), upper, preferred_element_type=f32) + carry
        ranks.append(upto - part)
        carry = jnp.broadcast_to(upto[:, 127:128], (PENS, 128))
    rank = jnp.concatenate(ranks, axis=1)
    over = jnp.where(jnp.max(carry, axis=0, keepdims=True) > SLOTS, 1.0, 0.0)
    over = jnp.concatenate([over] * (SLOTS // 128), axis=1)
    pos_first = jnp.sum(jnp.where(pen == owner, rank, 0.0), axis=0, keepdims=True)
    pos_second = jnp.sum(jnp.where(pen == owner + 1, rank, 0.0), axis=0, keepdims=True)
    pos_first = jnp.where(live > 0.0, pos_first, -1.0).astype(jnp.int32)
    pos_second = jnp.where(live > 0.0, pos_second, -1.0).astype(jnp.int32)
    route_ref[...] = jnp.zeros((8, count), jnp.int32)
    route_ref[0:1, :] = owner
    route_ref[1:2, :] = pos_first
    route_ref[2:3, :] = pos_second

    for ref in (first_ref, second_ref):
        ref[...] = jnp.zeros((ROWS, count), f32)
        ref[18:19, :] = q
        ref[19:20, :] = corner_ref[1:2, :].astype(f32)
        ref[20:21, :] = corner_ref[2:3, :].astype(f32)
        ref[21:22, :] = live
    w0 = stencil_ref[0:9, :]
    w1 = stencil_ref[9:18, :]
    w2 = stencil_ref[18:27, :]
    first_ref[0:9, :] = jnp.where(odd, 0.0, w0)
    first_ref[9:18, :] = jnp.where(odd, w0, w1)
    second_ref[0:9, :] = jnp.where(odd, w1, w2)
    second_ref[9:18, :] = jnp.where(odd, w2, 0.0)
    for ref in (first_ref, second_ref):
        w = ref[0:18, :]
        ref[24:42, :] = w - w.astype(bf16).astype(f32)

    step = 512
    total_ref[...] = jnp.zeros_like(total_ref)

    def chunk(k, _):
        at = pl.ds(pl.multiple_of(k * step, step), step)
        own = route_ref[0:1, at]
        slot = iota((SLOTS, step), 0)
        for ref, shift, row in ((first_ref, 0, 1), (second_ref, 1, 2)):
            values = ref[:, at].astype(bf16)
            spread = jnp.concatenate(
                [
                    values * jnp.where(own + shift == p, 1.0, 0.0).astype(bf16)
                    for p in range(PENS)
                ],
                axis=0,
            )
            hot = jnp.where(slot == route_ref[row : row + 1, at], 1.0, 0.0).astype(bf16)
            total_ref[...] += lax.dot_general(spread, hot, NT, preferred_element_type=f32)
        return 0

    lax.fori_loop(0, count // step, chunk, 0)
    first_ref[...] = jnp.zeros_like(first_ref)
    first_ref[22:23, 0:SLOTS] = over
    first_ref[42:48, 0:CAP] = charge[0:6]
    for k in range(4):
        half = slice(k % 2 * 128, k % 2 * 128 + 128)
        first_ref[42 + k : 43 + k, CAP:SLOTS] = charge[6 + k // 2 : 7 + k // 2, half]
    extra = first_ref[:, 0:SLOTS]
    for p in range(PENS):
        out_ref[p] = (total_ref[ROWS * p : ROWS * p + ROWS, :] + extra).astype(bf16)


def rows_as_bf16():
    return iota((M, TILE), 0).astype(f32).astype(bf16)


def hot_z(z, c):
    one = jnp.ones((M, TILE), bf16)
    return jnp.where(rows_as_bf16() == (z + c).astype(f32).astype(bf16), one, jnp.zeros_like(one))


def deposit_kernel(
    recv_ref, table_ref, out_ref, packed_ref, meta_ref, left_ref, right_ref,
    low_ref, grid_ref,
):
    packed_ref[...] = jnp.zeros_like(packed_ref)
    blocks = [recv_ref[s].astype(f32) for s in range(PENS)]
    counts = [jnp.sum(b[21:22, :]).astype(jnp.int32) for b in blocks]
    start = jnp.int32(0)
    for s in range(PENS):
        meta_ref[s] = start
        block = blocks[s][:FIELDS] + jnp.concatenate(
            [blocks[s][FIELDS : FIELDS + 18], jnp.zeros((FIELDS - 18, SLOTS), f32)], axis=0
        )
        block = jnp.concatenate([block, jnp.zeros((FIELDS, 128), f32)], axis=1)
        block = pltpu.roll(block, start % 128, 1)
        at = pl.ds(pl.multiple_of(start // 128 * 128, 128), SLOTS + 128)
        packed_ref[:, at] = packed_ref[:, at] + block
        start = start + counts[s]
    meta_ref[PENS] = start
    over = blocks[0][22:23, :128]
    for s in range(1, PENS):
        over = jnp.maximum(over, blocks[s][22:23, :128])
    spoil = jnp.where(over[:, :1] > 0.0, jnp.nan, 0.0)
    grid_ref[...] = jnp.zeros_like(grid_ref)

    def tile(r, _):
        fields = packed_ref[:, pl.ds(pl.multiple_of(r * TILE, TILE), TILE)]
        y = fields[19:20].astype(jnp.int32)
        z = fields[20:21].astype(jnp.int32)
        weights = fields[0:18] * fields[18:19]
        high = weights.astype(bf16)
        low = (weights - high.astype(f32)).astype(bf16)
        place = rows_as_bf16()
        at0, at1, at2 = [place == (y + b).astype(f32).astype(bf16) for b in range(3)]
        zero = jnp.zeros((M, TILE), bf16)
        for c in range(3):
            left_ref[:, c * TILE : (c + 1) * TILE] = hot_z(z, c)
            for xp in range(2):
                for part, ref in ((high, right_ref), (low, low_ref)):
                    w = [part[xp * 9 + b * 3 + c : xp * 9 + b * 3 + c + 1] for b in range(3)]
                    v = jnp.where(at0, w[0], jnp.where(at1, w[1], jnp.where(at2, w[2], zero)))
                    ref[xp * M : (xp + 1) * M, c * TILE : (c + 1) * TILE] = v
        left = left_ref[...]
        grid_ref[...] += lax.dot_general(
            left, right_ref[...], NT, preferred_element_type=f32
        ) + lax.dot_general(left, low_ref[...], NT, preferred_element_type=f32)
        return 0

    lax.fori_loop(0, (start + TILE - 1) // TILE, tile, 0)
    grid = grid_ref[...] + spoil
    high = grid.astype(bf16)
    low = (grid - high.astype(f32)).astype(bf16)
    for k in range(4):
        at = slice(k * 256, k * 256 + 256)
        table = table_ref[at, :]
        out_ref[at, :] = (
            jnp.dot(table, high, preferred_element_type=f32)
            + jnp.dot(table, low, preferred_element_type=f32)
        ).astype(bf16)


def recut_kernel(slab_ref, green_ref, *out_refs):
    for s, ref in enumerate(out_refs):
        first = (slab_ref[0] + s) % 8 * 4
        for c in range(4):
            ref[c] = green_ref[pl.ds(first + c, L // 8, stride=32), :].astype(bf16)


def convolve_kernel(
    slab_ref, recv_ref, g0_ref, g1_ref, g2_ref, g3_ref, g4_ref, g5_ref, g6_ref, g7_ref, along_y_ref, along_x_ref, back_y_ref, back_x_ref, out_ref, in_ref, sum_ref, green_ref
):
    j = pl.program_id(0)

    @pl.when(j == 0)
    def _():
        for h in range(4):
            in_ref[h] = recv_ref[:, h * 128 : h * 128 + 128].astype(f32)

    for s, ref in enumerate((g0_ref, g1_ref, g2_ref, g3_ref, g4_ref, g5_ref, g6_ref, g7_ref)):
        for i in range(4):
            green_ref[i, (slab_ref[0] + 8 - s) % 8] = ref[i]

    def piece(i, xp):
        return jnp.concatenate(
            [
                in_ref[2 * xp + h, pl.ds(8 * j + 2 * i + c, DEVS, stride=8), :].astype(bf16)
                for c in range(2)
                for h in range(2)
            ],
            axis=1,
        )

    both = [jnp.concatenate([piece(i, 0), piece(i, 1)], axis=0) for i in range(4)]
    both = [
        lax.dot_general(along_y_ref[...], t, NT, preferred_element_type=f32).astype(bf16)
        for t in both
    ]
    both = [
        jnp.dot(
            jnp.concatenate([t[:L], t[L:]], axis=1),
            along_x_ref[...],
            preferred_element_type=f32,
        )
        for t in both
    ]
    greens = [green_ref[i].reshape(L, L).astype(f32) for i in range(4)]
    both = [
        jnp.concatenate([(t[:, :L] * g).astype(bf16), (t[:, L:] * g).astype(bf16)], axis=0)
        for t, g in zip(both, greens)
    ]
    both = [
        jnp.dot(back_y_ref[...], t, preferred_element_type=f32).astype(bf16) for t in both
    ]
    both = [
        lax.dot_general(
            back_x_ref[...],
            jnp.concatenate([t[:M], t[M:]], axis=1),
            NT,
            preferred_element_type=f32,
        )
        for t in both
    ]
    for i in range(4):
        for c in range(2):
            for xp in range(2):
                row = c * M + xp * DEVS
                for h in range(2):
                    sum_ref[2 * xp + h, pl.ds(8 * j + 2 * i + c, DEVS, stride=8), :] = both[i][
                        row : row + DEVS, h * 128 : h * 128 + 128
                    ]

    @pl.when(j == 0)
    def _():
        for h in range(4):
            out_ref[:, h * 128 : h * 128 + 128] = sum_ref[h].astype(bf16)


def interpolate_kernel(meta_ref, recv_ref, table_ref, packed_ref, out_ref, flag_ref, grid_ref, result_ref):
    grid = jnp.dot(table_ref[...], recv_ref[...], preferred_element_type=f32)
    flag_ref[...] = jnp.where(jnp.isnan(grid[:8, :128]), 1.0, 0.0)
    grid = grid.T
    high = grid.astype(bf16)
    grid_ref[0] = high
    grid_ref[1] = (grid - high.astype(f32)).astype(bf16)
    result_ref[...] = jnp.zeros_like(result_ref)

    def tile(r, _):
        at = pl.ds(pl.multiple_of(r * TILE, TILE), TILE)
        fields = packed_ref[:, at]
        y = fields[19:20].astype(jnp.int32)
        z = fields[20:21].astype(jnp.int32)
        away = iota((M, TILE), 0) - y
        is0, is1, is2 = away == 0, away == 1, away == 2
        total = jnp.zeros((M, TILE), f32)
        for c in range(3):
            hot = hot_z(z, c)
            near = jnp.dot(grid_ref[0], hot, preferred_element_type=f32) + jnp.dot(
                grid_ref[1], hot, preferred_element_type=f32
            )
            for xp in range(2):
                w = [fields[xp * 9 + b * 3 + c : xp * 9 + b * 3 + c + 1] for b in range(3)]
                v = jnp.where(is0, w[0], jnp.where(is1, w[1], jnp.where(is2, w[2], 0.0)))
                total = total + v * near[xp * M : (xp + 1) * M]
        result_ref[:, at] = jnp.broadcast_to(jnp.sum(total, axis=0, keepdims=True), (8, TILE))
        return 0

    lax.fori_loop(0, (meta_ref[PENS] + TILE - 1) // TILE, tile, 0)
    width = SLOTS + 128
    for s in range(PENS):
        start = meta_ref[s]
        piece = result_ref[:, pl.ds(pl.multiple_of(start // 128 * 128, 128), width)]
        piece = pltpu.roll(piece, (width - start % 128) % width, 1)
        out_ref[s : s + 1, :] = piece[0:1, :SLOTS]


def collect_kernel(back_ref, route_ref, out_ref):
    back = back_ref[...]
    high = back.astype(bf16)
    low = (back - high.astype(f32)).astype(bf16)
    both = jnp.concatenate([high.astype(f32), low.astype(f32)], axis=0).astype(bf16)
    step = 512
    for k in range(4):
        at = slice(k * step, k * step + step)
        owner = route_ref[0:1, at]
        slot = iota((SLOTS, step), 0)
        pen = iota((PENS, step), 0)
        total = jnp.zeros((PENS, step), f32)
        for shift in range(2):
            hot = jnp.where(slot == route_ref[shift + 1 : shift + 2, at], 1.0, 0.0).astype(bf16)
            got = jnp.dot(both, hot, preferred_element_type=f32)
            total = total + jnp.where(pen == owner + shift, got[:PENS] + got[PENS:], 0.0)
        out_ref[:, at] = jnp.broadcast_to(jnp.sum(total, axis=0, keepdims=True), (8, step))


def struct(shape, dtype):
    return jax.ShapeDtypeStruct(shape, dtype)


def whole(count):
    return [pl.BlockSpec(memory_space=pltpu.VMEM)] * count


SMEM = pl.BlockSpec(memory_space=pltpu.SMEM)
LIMIT = pltpu.CompilerParams(vmem_limit_bytes=40 * 1024 * 1024)


def far_field_blocks(charges, stencil, corner_cells, cluster_sizes, green_spectrum):
    along_z, along_y, along_x, back_y, back_x, back_z = [jnp.asarray(t) for t in tables()]
    slab = lax.axis_index("clus").astype(jnp.int32).reshape(1)
    green = green_spectrum.transpose(1, 2, 0).reshape(-1, L)
    sent, route = pl.pallas_call(
        bucket_kernel,
        out_shape=[
            struct((PENS, ROWS, SLOTS), bf16),
            struct((8, 8 * CAP), jnp.int32),
        ],
        in_specs=[SMEM, SMEM] + whole(3),
        out_specs=whole(2),
        scratch_shapes=[
            pltpu.VMEM((ROWS, 8 * CAP), f32),
            pltpu.VMEM((ROWS, 8 * CAP), f32),
            pltpu.VMEM((ROWS * PENS, SLOTS), f32),
        ],
        compiler_params=LIMIT,
        name="bucket",
    )(
        slab,
        cluster_sizes,
        charges.reshape(8, CAP),
        stencil,
        corner_cells,
    )
    green, sent = lax.optimization_barrier((green, sent))
    pieces = pl.pallas_call(
        recut_kernel,
        grid=(4,),
        out_shape=[struct((4, L // 8, L), bf16)] * 8,
        in_specs=[SMEM, pl.BlockSpec((L // 8 * 32, 128), lambda j: (0, j))],
        out_specs=[pl.BlockSpec((4, L // 8, 128), lambda j: (0, 0, j))] * 8,
        compiler_params=LIMIT,
        name="recut",
    )(slab, green)
    recv = lax.all_to_all(sent, "pen", 0, 0, tiled=True)
    pieces = [pieces[0]] + [
        lax.ppermute(pieces[s], "clus", [(a, (a + s) % 8) for a in range(8)])
        for s in range(1, 8)
    ]
    section, packed, meta = pl.pallas_call(
        deposit_kernel,
        out_shape=[
            struct((2 * L, 2 * M), bf16),
            struct((FIELDS, ROOM), f32),
            struct((PENS + 1,), jnp.int32),
        ],
        in_specs=whole(2),
        out_specs=whole(2) + [SMEM],
        scratch_shapes=[
            pltpu.VMEM((M, 3 * TILE), bf16),
            pltpu.VMEM((2 * M, 3 * TILE), bf16),
            pltpu.VMEM((2 * M, 3 * TILE), bf16),
            pltpu.VMEM((M, 2 * M), f32),
        ],
        compiler_params=LIMIT,
        name="deposit",
    )(recv, along_z)
    section, *pieces = lax.optimization_barrier((section, *pieces))
    section = lax.all_to_all(
        section.reshape(DEVS, 8, 2 * M), ("clus", "pen"), 0, 0, tiled=True
    )
    section = pl.pallas_call(
        convolve_kernel,
        grid=(1,),
        out_shape=struct((2 * L, 2 * M), bf16),
        in_specs=[
            SMEM,
            pl.BlockSpec((2 * L, 2 * M), lambda j: (0, 0)),
        ]
        + [pl.BlockSpec((4, L // 8, L), lambda j: (j, 0, 0))] * 8
        + [
            pl.BlockSpec((2 * L, 2 * M), lambda j: (0, 0)),
            pl.BlockSpec((2 * M, 2 * L), lambda j: (0, 0)),
            pl.BlockSpec((2 * M, 2 * L), lambda j: (0, 0)),
            pl.BlockSpec((2 * M, 2 * L), lambda j: (0, 0)),
        ],
        out_specs=pl.BlockSpec((2 * L, 2 * M), lambda j: (0, 0)),
        scratch_shapes=[
            pltpu.VMEM((4, 2 * L, 128), f32),
            pltpu.VMEM((4, 2 * L, 128), f32),
            pltpu.VMEM((4, 8, L // 8, L), bf16),
        ],
        compiler_params=LIMIT,
        name="convolve",
    )(slab, section.reshape(2 * L, 2 * M), *pieces, along_y, along_x, back_y, back_x)
    section = lax.all_to_all(
        section.reshape(DEVS, 8, 2 * M), ("clus", "pen"), 0, 0, tiled=True
    )
    back, flag = pl.pallas_call(
        interpolate_kernel,
        out_shape=[struct((PENS, SLOTS), f32), struct((8, 128), f32)],
        in_specs=[SMEM] + whole(3),
        out_specs=whole(2),
        scratch_shapes=[pltpu.VMEM((2, 2 * M, M), bf16), pltpu.VMEM((8, ROOM), f32)],
        compiler_params=LIMIT,
        name="interpolate",
    )(meta, section.reshape(2 * L, 2 * M), back_z, packed)
    back = lax.all_to_all(back, "pen", 0, 0, tiled=True)
    far = pl.pallas_call(
        collect_kernel,
        out_shape=struct((8, 8 * CAP), f32),
        in_specs=whole(2),
        out_specs=pl.BlockSpec(memory_space=pltpu.VMEM),
        compiler_params=LIMIT,
        name="collect",
    )(back, route)
    pool = jnp.concatenate(
        [recv[:, 42:48, :CAP], recv[:, 42:46, CAP:].reshape(PENS, 2, CAP)], axis=1
    ).reshape(PENS * 8, CAP)
    return far[0], pool, flag[0, 0]


def neighbours(x, axis):
    devices = lax.axis_size(axis)
    up = [(i, i + 1) for i in range(devices - 1)]
    before = lax.ppermute(x, axis, up)
    after = lax.ppermute(x, axis, [(j, i) for i, j in up])
    return jnp.concatenate([before, x, after], axis=0)


def per_device(
    charges, stencil, corner_cells, cluster_sizes, near_source, near_blocks, green_spectrum
):
    slot_rank = jnp.arange(CAP, dtype=jnp.int32)
    slot_mask = (slot_rank[None, :] < cluster_sizes[:, None]).reshape(-1)
    far_field, pool, overflow = far_field_blocks(
        charges, stencil, corner_cells, cluster_sizes, green_spectrum
    )
    local_source = near_source - (lax.axis_index("clus") - 1) * pool.shape[0]
    source_rows = neighbours(pool, "clus")[local_source]
    near_terms = jnp.einsum(
        "pjm,pm->pj", near_blocks, source_rows, preferred_element_type=f32
    )
    near_field = near_terms.reshape(-1, NB, CAP).sum(axis=1).reshape(-1)

    def general():
        charge_value = jnp.where(slot_mask, charges, jnp.zeros_like(charges)).astype(f32)
        return far_field_general(charge_value, stencil, corner_cells, green_spectrum)

    far_field = lax.cond(overflow > 0.0, general, lambda: far_field)
    total = far_field + near_field
    return jnp.where(slot_mask, total, jnp.zeros_like(total))


def solution(mesh):
    in_specs = (
        P(("clus", "pen")),
        P(None, ("clus", "pen")),
        P(None, ("clus", "pen")),
        P(("clus", "pen")),
        P(("clus", "pen")),
        P(("clus", "pen"), None, None),
        P(None, "clus", "pen"),
    )
    out_specs = P(("clus", "pen"))
    return jax.shard_map(
        per_device, mesh=mesh, in_specs=in_specs, out_specs=out_specs, check_vma=False
    )
```
